32 devices in a mesh: groups: 2 (over x), tok: 16 (over z, y, core).
Axes of the slice: x: 2, y: 2, z: 4, core: 2. Of those that a mesh axis runs over, the one named last changes fastest.
Arguments:
- tokens: bfloat16 [8192, 1024], P(('groups', 'tok')), parts along dimension 0, may hold values from -6 to 6
- norm_gain: float32 [1024], replicated, may hold values from 0.1 to 1.9
- w_qk: bfloat16 [1024, 1024], replicated, may hold values from -0.1875 to 0.1875
- w_v: bfloat16 [1024, 1024], replicated, may hold values from -0.1875 to 0.1875
- cotangent: bfloat16 [8192, 1024], P(('groups', 'tok')), parts along dimension 0, may hold values from -48 to 48
- log_sums: float32 [2, 8, 8192], P(None, None, ('groups', 'tok')), parts along dimension 2, may hold values from 7 to 8
- bucket_order: int32 [2, 8192], P(None, 'groups'), parts along dimension 1, may hold values from 0 to 4095, as said below
- token_position: int32 [2, 8192], P(None, ('groups', 'tok')), parts along dimension 1, may hold values from 0 to 4095, as said below
Outputs:
- d_tokens: bfloat16 [8192, 1024], P(('groups', 'tok')), parts along dimension 0
- d_gain: float32 [2048], P(('groups', 'tok')), parts along dimension 0
- d_wqk: float32 [2048, 1024], P(('groups', 'tok')), parts along dimension 0
- d_wv: float32 [2048, 1024], P(('groups', 'tok')), parts along dimension 0
The draws below stay inside these ranges and needn't reach their ends.
There are 2 independent parts, one for each index of `groups`. The reference program is written for one: setup_inputs(seed, part) draws one part's arguments, and reference() takes and returns one part's arrays. A program takes and returns all parts, laid end to end along the dimension named above; an argument that names none is the same for every part. Nothing has to cross between parts.
Inputs may be any that keep to these rules, and one draw needn't show every extreme that they name: `bucket_order`: each row is a permutation; the 256 hash-sorted positions of one device hold at most 20 tokens of any one device's 256 tokens, and exactly 20 of at least one. token_position[r, bucket_order[r, p]] = p.
All inputs are finite; a program needn't handle non-finite values.
Results may differ from the reference program's by a relative error of at most 0.025.
Values may be sent and summed in bfloat16 or wider, within the bound.
No kernel may reach another device: no remote copies, remote signals or barrier semaphores. Data moves between devices by JAX's collectives and lax.ppermute only.
A program may use at most 128 MiB of HBM per device.

```python
import math
import jax
import jax.numpy as jnp
from jax import lax

H = 8
DH = 128
D = 1024
BLOCK = 256
ROUNDS = 2
TOK_DEV = 256
TOKENS = 4096
CAP = 20
N_TOK = 16


def build_orderings(key):
    orderings = []
    for hashing in range(ROUNDS):
        round_key = jax.random.fold_in(key, 7001 + hashing)
        device_key, jitter_key, source_key, target_key, tie_key = jax.random.split(round_key, 5)
        spare_rows = TOK_DEV - CAP
        base_load = spare_rows // (N_TOK - 1)
        extra_rows = spare_rows % (N_TOK - 1)
        placed = jax.random.permutation(device_key, N_TOK).astype(jnp.int32)
        jitter = jax.random.randint(jitter_key, (N_TOK - 1,), 0, base_load // 4 + 1).astype(jnp.int32)
        weights = base_load + (jnp.arange(N_TOK - 1) < extra_rows).astype(jnp.int32) + jitter - jnp.roll(jitter, -1)
        weights = jnp.concatenate([jnp.array([CAP], jnp.int32), weights.astype(jnp.int32)])
        source_ids = jnp.broadcast_to(jnp.arange(N_TOK, dtype=jnp.int32)[:, None], (N_TOK, N_TOK))
        offsets = jnp.broadcast_to(jnp.arange(N_TOK, dtype=jnp.int32)[None, :], (N_TOK, N_TOK))
        target = placed[(source_ids + offsets) % N_TOK]
        pair_loads = jnp.zeros((N_TOK, N_TOK), jnp.int32).at[source_ids, target].set(jnp.broadcast_to(weights[None, :], (N_TOK, N_TOK)))

        def spread(row_load, subkey):
            listed = jnp.repeat(jnp.arange(N_TOK, dtype=jnp.int32), row_load, total_repeat_length=TOK_DEV)
            return jax.random.permutation(subkey, listed)
        token_dest = jax.vmap(spread)(pair_loads, jax.random.split(source_key, N_TOK)).reshape(-1).astype(jnp.int32)
        slot_source = jax.vmap(spread)(pair_loads.T, jax.random.split(target_key, N_TOK)).reshape(-1).astype(jnp.int32)
        tiebreak = jax.random.permutation(tie_key, TOKENS).astype(jnp.int32)
        block_ids = (jnp.arange(TOKENS, dtype=jnp.int32) // TOK_DEV).astype(jnp.int32)
        token_score = (token_dest * N_TOK + block_ids) * TOKENS + tiebreak
        place_score = (block_ids * N_TOK + slot_source) * TOKENS + jnp.arange(TOKENS, dtype=jnp.int32)
        token_sorted = jnp.argsort(token_score, stable=True).astype(jnp.int32)
        place_sorted = jnp.argsort(place_score, stable=True).astype(jnp.int32)
        ordering = jnp.zeros((TOKENS,), jnp.int32).at[place_sorted].set(token_sorted)
        orderings.append(ordering)
    return jnp.stack(orderings)


def draw_bucket_order(key, part):
    return build_orderings(key)


def draw_token_position(key, part):
    orderings = build_orderings(key)
    places = jnp.arange(TOKENS, dtype=jnp.int32)
    return jnp.stack([jnp.zeros((TOKENS,), jnp.int32).at[orderings[hashing]].set(places) for hashing in range(ROUNDS)])


def spiked(drawn, stream_key, source, target, blocks, factor):
    owner, partner = [(jnp.arange(drawn.shape[position]) // (drawn.shape[position] // blocks)).reshape([-1 if axis == position else 1 for axis in range(drawn.ndim)]) for position in (source, target)]
    chosen = jax.random.permutation(stream_key, blocks)[partner]
    strong = (owner == chosen) | (owner == (partner + blocks // 2) % blocks)
    return jnp.where(strong, factor * drawn, drawn)


def shard_levels(rng, extent, cuts, least, largest):
    factor_of = 1.0
    for dim, parts in cuts:
        steps = jax.random.uniform(jax.random.fold_in(jax.random.fold_in(rng, 6), dim), (parts,), jnp.float32, least / len(cuts), largest / len(cuts))
        factor_of = factor_of * jnp.repeat(jnp.exp(steps), extent[dim] // parts).reshape((-1,) + (1,) * (len(extent) - 1 - dim))
    return factor_of


def scatter_about(key, shape, width, reach, cuts=(), held_as=jnp.bfloat16):
    values = jax.random.normal(key, shape, jnp.float32) * width
    if len(cuts) > 0:
        values = shard_levels(key, shape, cuts, -0.22, 0.18) * values
    return jnp.clip(values, min=-reach, max=reach).astype(held_as)


def noise_with(own_key, shape, deviation, reach, cuts, heavy, held_as=jnp.bfloat16):
    drawn = deviation * jax.random.normal(own_key, shape, jnp.float32)
    if cuts:
        drawn = drawn * shard_levels(own_key, shape, cuts, -0.22, 0.18)
    return jnp.clip(spiked(drawn, jax.random.fold_in(own_key, 3), *heavy), -reach, reach).astype(held_as)


def setup_inputs(seed: int = 0, part: int = 0) -> dict:
    key_of = jax.random.split(jax.random.key(seed), 9)
    own_keys = jax.random.split(jax.random.fold_in(key_of[8], part), 9)
    return {
        "tokens": noise_with(own_keys[0], (TOKENS, D), 1.0, 6.0, ((0, 16),), (0, 1, 16, 2.0)),
        "norm_gain": jnp.clip(1.0 + 0.18 * jax.random.normal(key_of[1], (D,), jnp.float32), 0.1, 1.9),
        "w_qk": scatter_about(key_of[2], (D, D), D ** -0.5, 0.1875),
        "w_v": scatter_about(key_of[3], (D, D), D ** -0.5, 0.1875),
        "cotangent": scatter_about(own_keys[4], (TOKENS, D), 8.0, 48.0, ((0, 16),)),
        "log_sums": jnp.clip(7.0 + 1.0 * jax.random.uniform(own_keys[5], (ROUNDS, H, TOKENS), jnp.float32) ** shard_levels(own_keys[5], (ROUNDS, H, TOKENS), ((2, 16),), -0.2, 0.2), 7.0, 8.0),
        "bucket_order": draw_bucket_order(jax.random.fold_in(jax.random.fold_in(key_of[8], part), 71), part),
        "token_position": draw_token_position(jax.random.fold_in(jax.random.fold_in(key_of[8], part), 71), part),
    }


def normed(values, scales):
    return values * lax.rsqrt(lax.optimization_barrier(jnp.mean(values * values, axis=-1, keepdims=True)) + 1e-06) * scales

def unit_keys(queries):
    head_depth = queries.shape[-1]
    return queries * lax.rsqrt(lax.optimization_barrier(jnp.mean(queries * queries, axis=-1, keepdims=True)) + 1e-06) / math.sqrt(head_depth)

def attend(queries, keys_all, values_all, out_grads, log_sum):
    block_len = queries.shape[1]
    queries_f = queries.astype(jnp.float32)
    keys_f = keys_all.astype(jnp.float32)
    values_f = values_all.astype(jnp.float32)
    grads_f = out_grads.astype(jnp.float32)
    scores = jnp.einsum('cihe,cjhe->chij', queries_f, keys_f)
    diagonal = jnp.arange(2 * block_len)[None, :] == jnp.arange(block_len)[:, None] + block_len
    weights = jnp.where(diagonal, 0.0, jnp.exp(scores - log_sum[:, :, :, None]))
    d_weights = jnp.einsum('cihe,cjhe->chij', grads_f, values_f)
    totals = lax.optimization_barrier(jnp.sum(weights * d_weights, axis=-1, keepdims=True))
    d_scores = (weights * (d_weights - totals)).astype(jnp.bfloat16).astype(jnp.float32)
    weights_low = weights.astype(jnp.bfloat16).astype(jnp.float32)
    d_values = jnp.einsum('chij,cihe->cjhe', weights_low, grads_f)
    d_queries = jnp.einsum('chij,cjhe->cihe', d_scores, keys_f)
    d_keys = jnp.einsum('chij,cihe->cjhe', d_scores, queries_f)
    return (d_queries, d_keys, d_values)

def one_block(members):
    results = attend(*[member[None] for member in members])
    return tuple((result[0] for result in results))

def reference(tokens, norm_gain, w_qk, w_v, cotangent, log_sums, bucket_order, token_position):
    tokens_wide = tokens.astype(jnp.float32)
    normal_rows = normed(tokens_wide, norm_gain).astype(jnp.bfloat16)
    query_rows = jnp.dot(normal_rows, w_qk, preferred_element_type=jnp.float32).astype(jnp.bfloat16)
    value_rows = jnp.dot(normal_rows, w_v, preferred_element_type=jnp.float32).astype(jnp.bfloat16)
    block_count = TOKENS // BLOCK
    d_normal = jnp.zeros((TOKENS, D), jnp.float32)
    grad_qk = jnp.zeros((D, D), jnp.float32)
    grad_v = jnp.zeros((D, D), jnp.float32)
    for hashing in range(ROUNDS):
        order_row = bucket_order[hashing]
        query_four = query_rows[order_row].reshape(block_count, BLOCK, H, DH)
        value_four = value_rows[order_row].reshape(block_count, BLOCK, H, DH)
        grad_four = cotangent[order_row].reshape(block_count, BLOCK, H, DH)
        unit_four = unit_keys(query_four.astype(jnp.float32)).astype(jnp.bfloat16)
        block_sums = log_sums[hashing].reshape(H, block_count, BLOCK).transpose(1, 0, 2)
        keys_all = jnp.concatenate([jnp.roll(unit_four, 1, axis=0), unit_four], axis=1)
        values_all = jnp.concatenate([jnp.roll(value_four, 1, axis=0), value_four], axis=1)
        d_query, d_keys, d_values = lax.map(one_block, (query_four, keys_all, values_all, grad_four, block_sums))
        key_grad = d_keys[:, BLOCK:] + jnp.roll(d_keys[:, :BLOCK], -1, axis=0)
        value_grad = d_values[:, BLOCK:] + jnp.roll(d_values[:, :BLOCK], -1, axis=0)
        _, key_pull = jax.vjp(unit_keys, query_four.astype(jnp.float32))
        query_grad = d_query + key_pull(key_grad)[0]
        places = token_position[hashing]
        query_low = query_grad.reshape(TOKENS, D).astype(jnp.bfloat16)[places]
        value_low = value_grad.reshape(TOKENS, D).astype(jnp.bfloat16)[places]
        grad_qk = grad_qk + jnp.dot(normal_rows.T, query_low, preferred_element_type=jnp.float32)
        grad_v = grad_v + jnp.dot(normal_rows.T, value_low, preferred_element_type=jnp.float32)
        d_normal = d_normal + jnp.dot(query_low, w_qk.T, preferred_element_type=jnp.float32) + jnp.dot(value_low, w_v.T, preferred_element_type=jnp.float32)
    _, norm_pull = jax.vjp(normed, tokens_wide, norm_gain)
    d_tokens, grad_gain = norm_pull(d_normal)
    grad_scale = 1.0 / math.sqrt(TOKENS)
    return (d_tokens.astype(jnp.bfloat16), grad_gain * grad_scale, grad_qk * grad_scale, grad_v * grad_scale)
```

```python
import math
from functools import partial

import jax
import jax.numpy as jnp
from jax import lax
from jax.experimental import pallas as pl
from jax.experimental.pallas import tpu as pltpu
from jax.sharding import PartitionSpec as P

BLOCK = 256
EPS = 1e-06
F32 = jnp.float32
BF16 = jnp.bfloat16
TILE = 8
NN = (((1,), (0,)), ((), ()))
NT = (((1,), (1,)), ((), ()))
TN = (((0,), (0,)), ((), ()))
VMEM_BYTES = 60 * 1024 * 1024


def dot(a, b, dims):
    return lax.dot_general(a, b, dims, preferred_element_type=F32)


def every(lead, size):
    return pl.ds(lead, size, stride=TILE)


def attention_kernel(
    per, parts, blocks, rounds, ids, order, log_sums, *refs
):
    qv_refs = refs[:per]
    cot_refs = refs[per : 2 * per]
    out_refs = refs[2 * per : 3 * per]
    table, picked, packed, keys, values, queries, dq, dk, dv = refs[3 * per :]
    chips = qv_refs[0].shape[0]
    size = qv_refs[0].shape[1]
    head_dim = cot_refs[0].shape[-1]
    total = table.shape[0] // TILE
    block_total = total // BLOCK
    first_block = ids[4, 0]

    for m in range(per):

        def fill(n, carry):
            base = (ids[0, n] * per + ids[3, m]) * (size * TILE)
            table[every(base, size), :] = qv_refs[m][n, :, :head_dim].astype(F32)
            table[every(base + 1, size), :] = qv_refs[m][n, :, head_dim:].astype(F32)
            base = (ids[1, n] * per + ids[3, m]) * (size * TILE)
            table[every(base + 2, size), :] = cot_refs[m][n].astype(F32)
            if parts > 1:
                zero = jnp.zeros((size, head_dim), F32)
                table[every(base + 3, size), :] = zero
                table[every(base + 4, size), :] = zero
            return carry

        lax.fori_loop(0, chips, fill, 0)

    def gather(block):
        start = block * BLOCK

        def body(step, carry):
            for u in range(32):
                p = step * 32 + u
                row = pl.multiple_of(order[start + p] * TILE, TILE)
                picked[pl.ds(pl.multiple_of(p * TILE, TILE), TILE), :] = table[pl.ds(row, TILE), :]
            return carry

        lax.fori_loop(0, BLOCK // 32, body, 0)

    def scatter(block):
        start = block * BLOCK

        def body(step, carry):
            for u in range(32):
                p = step * 32 + u
                row = pl.multiple_of(order[start + p] * TILE, TILE)
                table[pl.ds(row, TILE), :] = packed[pl.ds(pl.multiple_of(p * TILE, TILE), TILE), :]
            return carry

        lax.fori_loop(0, BLOCK // 32, body, 0)

    def load(slot):
        q = picked[every(0, BLOCK), :]
        scale = lax.rsqrt(jnp.mean(q * q, axis=-1, keepdims=True) + EPS) * (1.0 / math.sqrt(head_dim))
        queries[slot] = q
        keys[slot] = (q * scale).astype(BF16)
        values[slot] = picked[every(1, BLOCK), :].astype(BF16)

    def finish(slot, block):
        q = queries[slot]
        d_key = dk[slot]
        scale = lax.rsqrt(jnp.mean(q * q, axis=-1, keepdims=True) + EPS)
        inner = jnp.mean(q * d_key, axis=-1, keepdims=True)
        pulled = (scale * (1.0 / math.sqrt(head_dim))) * (d_key - q * (scale * scale * inner))
        packed[every(3, BLOCK), :] = dq[slot] + pulled
        packed[every(4, BLOCK), :] = dv[slot]
        scatter(block)

    halo_block = lax.rem(first_block + block_total - 1, block_total)
    gather(halo_block)
    load(2)
    dk[2] = jnp.zeros_like(dk[2])
    dv[2] = jnp.zeros_like(dv[2])
    dq[2] = jnp.zeros_like(dq[2])

    row_id = lax.broadcasted_iota(jnp.int32, (BLOCK, BLOCK), 0)
    col_id = lax.broadcasted_iota(jnp.int32, (BLOCK, BLOCK), 1)
    diagonal = row_id == col_id

    def step(b, carry):
        block = first_block + b
        cur = lax.rem(b, 2)
        prev = jnp.where(b == 0, 2, 1 - cur)
        gather(block)
        load(cur)
        log_sum = log_sums[pl.ds(block, 1), :]
        cot = picked[every(2, BLOCK), :].astype(BF16)
        query = queries[cur].astype(BF16)
        key_a, key_b = keys[prev], keys[cur]
        w_a = jnp.exp(dot(key_a, query, NT) - log_sum)
        w_b = jnp.where(diagonal, 0.0, jnp.exp(dot(key_b, query, NT) - log_sum))
        dw_a = dot(values[prev], cot, NT)
        dw_b = dot(values[cur], cot, NT)
        delta = jnp.sum(w_a * dw_a + w_b * dw_b, axis=0, keepdims=True)
        ds_a = (w_a * (dw_a - delta)).astype(BF16)
        ds_b = (w_b * (dw_b - delta)).astype(BF16)
        dv[prev] = dv[prev] + dot(w_a.astype(BF16), cot, NN)
        dv[cur] = dot(w_b.astype(BF16), cot, NN)
        dk[prev] = dk[prev] + dot(ds_a, query, NN)
        dk[cur] = dot(ds_b, query, NN)
        dq[cur] = (dot(key_a, ds_a, TN) + dot(key_b, ds_b, TN)).T

        @pl.when(b > 0)
        def _():
            finish(prev, block - 1)

        return carry

    lax.fori_loop(0, blocks, step, 0)
    last = (blocks - 1) % 2
    if parts == 1:
        dk[last] = dk[last] + dk[2]
        dv[last] = dv[last] + dv[2]
    else:
        finish(2, halo_block)
    finish(last, first_block + blocks - 1)

    for m in range(per):

        def drain(n, carry):
            base = (ids[2, n] * per + ids[3, m]) * (size * TILE)
            out_refs[m][n, :, :head_dim] = table[every(base + 3, size), :].astype(BF16)
            out_refs[m][n, :, head_dim:] = table[every(base + 4, size), :].astype(BF16)
            return carry

        lax.fori_loop(0, chips, drain, 0)


def attention(per, parts, rounds, ids, order, log_sums, qv, cot):
    chips, size, width = qv[0].shape
    head_dim = width // 2
    total = order.shape[0]
    blocks = total // BLOCK // parts
    smem = pl.BlockSpec(memory_space=pltpu.SMEM)
    vmem = pl.BlockSpec(memory_space=pltpu.VMEM)
    return pl.pallas_call(
        partial(attention_kernel, per, parts, blocks, rounds),
        out_shape=[jax.ShapeDtypeStruct((chips, size, width), BF16)] * per,
        in_specs=[smem, smem, vmem] + [vmem] * (2 * per),
        out_specs=[vmem] * per,
        scratch_shapes=[
            pltpu.VMEM((total * TILE, head_dim), F32),
            pltpu.VMEM((BLOCK * TILE, head_dim), F32),
            pltpu.VMEM((BLOCK * TILE, head_dim), F32),
            pltpu.VMEM((3, BLOCK, head_dim), BF16),
            pltpu.VMEM((3, BLOCK, head_dim), BF16),
            pltpu.VMEM((3, BLOCK, head_dim), F32),
            pltpu.VMEM((3, BLOCK, head_dim), F32),
            pltpu.VMEM((3, BLOCK, head_dim), F32),
            pltpu.VMEM((3, BLOCK, head_dim), F32),
        ],
        compiler_params=pltpu.CompilerParams(vmem_limit_bytes=VMEM_BYTES),
        name="attention",
    )(ids, order, log_sums, *qv, *cot)


def home_kernel(grads, weights, tokens, gain, out):
    total = jnp.zeros(tokens.shape, F32)
    for head in range(grads.shape[0]):
        total = total + dot(grads[head], weights[head], NT)
    x = tokens[...].astype(F32)
    scale = lax.rsqrt(jnp.mean(x * x, axis=-1, keepdims=True) + EPS)
    scaled = total * gain[...]
    inner = jnp.mean(x * scaled, axis=-1, keepdims=True)
    out[...] = (scale * (scaled - x * (scale * scale * inner))).astype(BF16)


def home(grads, weights, tokens, gain):
    return pl.pallas_call(
        home_kernel,
        out_shape=jax.ShapeDtypeStruct(tokens.shape, BF16),
        compiler_params=pltpu.CompilerParams(vmem_limit_bytes=VMEM_BYTES),
        name="home",
    )(grads, weights, tokens, gain)


def per_device(tokens, norm_gain, w_qk, w_v, cotangent, log_sums, bucket_order, token_position):
    devices = lax.axis_size("tok")
    me = lax.axis_index("tok")
    size, width = tokens.shape
    rounds, heads, _ = log_sums.shape
    head_dim = width // heads
    total = bucket_order.shape[1]
    per = devices // heads
    parts = per // rounds
    chips = heads
    chip, lane = me // per, me % per
    hashing, part = lane % rounds, lane // rounds
    groups = [[c * per + j for c in range(chips)] for j in range(per)]
    ring = list(range(0, chips, 2)) + list(range(chips - 1, 0, -2))
    place = [ring.index(c) for c in range(chips)]

    def hop(x, distance):
        route = [
            (ring[p] * per + j, ring[(p + distance) % chips] * per + j)
            for p in range(chips)
            for j in range(per)
        ]
        return lax.ppermute(x, "tok", route)

    def swap(x, shift):
        route = [
            (c * per + j, c * per + (j + shift) % per) for c in range(chips) for j in range(per)
        ]
        return lax.ppermute(x, "tok", route)

    def exchange(x):
        return lax.all_to_all(x, "tok", 0, 0, tiled=True, axis_index_groups=groups)

    def by_head(x):
        return x.reshape(x.shape[0], heads, head_dim).transpose(1, 0, 2)

    sums_all = lax.all_gather(log_sums, "tok", axis=2, tiled=True)
    my_sums = lax.dynamic_slice(sums_all, (hashing, chip, 0), (1, 1, total)).reshape(-1, BLOCK)
    my_order = lax.dynamic_index_in_dim(bucket_order, hashing, 0, keepdims=False)

    x = tokens.astype(F32)
    normal = (
        x * lax.rsqrt(jnp.mean(x * x, axis=-1, keepdims=True) + EPS) * norm_gain
    ).astype(BF16)
    cot = exchange(by_head(cotangent))

    ring_ids = jnp.array(ring, jnp.int32)
    my_place = jnp.array(place, jnp.int32)[chip]
    shards, places = [normal], [my_place]
    ahead = behind = normal
    half = chips // 2
    for s in range(1, half):
        ahead, behind = hop(ahead, 1), hop(behind, -1)
        shards += [ahead, behind]
        places += [my_place - s, my_place + s]
    shards.append(
        jnp.concatenate([hop(ahead[: size // 2], 1), hop(behind[size // 2 :], -1)], axis=0)
    )
    places.append(my_place + half)
    shard_chips = ring_ids[jnp.stack(places) % chips]

    weights = jnp.concatenate(
        [
            w_qk.reshape(width, heads, head_dim).transpose(1, 0, 2),
            w_v.reshape(width, heads, head_dim).transpose(1, 0, 2),
        ],
        axis=2,
    )
    my_weights = lax.dynamic_index_in_dim(weights, chip, 0, keepdims=False)
    qv = jnp.stack(
        [jnp.dot(n, my_weights, preferred_element_type=F32).astype(BF16) for n in shards]
    )
    qv_all = [qv] + [swap(qv, shift) for shift in range(1, per)]
    cot_all = [cot] + [swap(cot, shift) for shift in range(1, per)]
    lanes = jnp.stack([(lane - shift) % per for shift in range(per)])

    def padded(v):
        return jnp.zeros((chips,), jnp.int32).at[: v.shape[0]].set(v.astype(jnp.int32))

    own_chips = jnp.arange(chips, dtype=jnp.int32)
    ids = jnp.stack(
        [
            shard_chips,
            own_chips,
            own_chips,
            padded(lanes),
            jnp.broadcast_to(part * (total // BLOCK // parts), (chips,)).astype(jnp.int32),
        ]
    )
    sent = attention(per, parts, rounds, ids, my_order, my_sums, qv_all, cot_all)
    grads = sent[0].astype(F32)
    for shift in range(1, per):
        grads = grads + swap(sent[shift], per - shift).astype(F32)
    grads = grads.astype(BF16)

    inbound = exchange(grads)
    normal_all = jnp.concatenate(shards, axis=0)
    grads_ring = grads[shard_chips].reshape(chips * size, 2 * head_dim)
    d_weights = jnp.einsum("td,te->de", normal_all, grads_ring, preferred_element_type=F32)
    rows = width // devices
    d_weights = d_weights.astype(BF16).reshape(chips, per, rows, 2 * head_dim)
    mine = lax.dynamic_index_in_dim(d_weights, lane, 1, keepdims=False).astype(F32)
    for shift in range(1, per):
        out = lax.dynamic_index_in_dim(d_weights, (lane + shift) % per, 1, keepdims=False)
        mine = mine + swap(out, shift).astype(F32)
    d_rows = exchange(mine.astype(BF16)).astype(F32) * (1.0 / math.sqrt(total))
    d_rows = d_rows.transpose(1, 0, 2)
    d_wqk = d_rows[:, :, :head_dim].reshape(rows, width)
    d_wv = d_rows[:, :, head_dim:].reshape(rows, width)

    d_tokens = home(inbound, weights, tokens, norm_gain[None, :])

    def own(v):
        return lax.dynamic_slice_in_dim(v, me * rows, rows, 0)

    weighted = d_wqk * own(w_qk).astype(F32) + d_wv * own(w_v).astype(F32)
    d_gain = jnp.sum(weighted, axis=1) / own(norm_gain)
    return d_tokens, d_gain, d_wqk, d_wv


def solution(mesh):
    in_specs = (
        P(("groups", "tok"), None),
        P(),
        P(),
        P(),
        P(("groups", "tok"), None),
        P(None, None, ("groups", "tok")),
        P(None, "groups"),
        P(None, ("groups", "tok")),
    )
    out_specs = (
        P(("groups", "tok"), None),
        P(("groups", "tok")),
        P(("groups", "tok"), None),
        P(("groups", "tok"), None),
    )
    return jax.shard_map(
        per_device, mesh=mesh, in_specs=in_specs, out_specs=out_specs, check_vma=False
    )
```

```python
import math
from functools import partial

import jax
import jax.numpy as jnp
import numpy as np
from jax import lax
from jax.experimental import pallas as pl
from jax.experimental.pallas import tpu as pltpu
from jax.sharding import PartitionSpec as P

BLOCK = 256
EPS = 1e-06
F32 = jnp.float32
BF16 = jnp.bfloat16
TILE = 8
NN = (((1,), (0,)), ((), ()))
NT = (((1,), (1,)), ((), ()))
TN = (((0,), (0,)), ((), ()))
VMEM_BYTES = 60 * 1024 * 1024
SMALL_VMEM_BYTES = 24 * 1024 * 1024
SHARDS, LANES = 0, 1


def dot(a, b, dims):
    return lax.dot_general(a, b, dims, preferred_element_type=F32)


def every(lead, size):
    return pl.ds(lead, size, stride=TILE)


def attention_kernel(per, parts, blocks, rounds, pieces, ids, order, *refs):
    qv_refs = [refs[m * pieces : (m + 1) * pieces] for m in range(per)]
    refs = refs[per * pieces :]
    cot_refs = refs[:per]
    out_refs = refs[per : 2 * per]
    table, picked, packed, log_sums, keys, values, queries, dq, dk, dv = refs[2 * per :]
    chips, size, width = out_refs[0].shape
    head_dim = width // 2
    total = table.shape[0] // TILE
    block_total = total // BLOCK
    sum_rows = size // head_dim
    lo_start = rounds * sum_rows
    hashing = ids[LANES, per]
    first_block = ids[LANES, per + 1]

    for m in range(per):
        n = 0
        for ref in qv_refs[m]:
            for row in range(ref.shape[0]):
                base = (ids[SHARDS, n] * per + ids[LANES, m]) * (size * TILE)
                table[every(base, size), :] = ref[row, :, :head_dim].astype(F32)
                table[every(base + 1, size), :] = ref[row, :, head_dim:].astype(F32)
                n += 1

        def fill(n, carry):
            device = n * per + ids[LANES, m]
            base = device * (size * TILE)
            table[every(base + 2, size), :] = cot_refs[m][n, :size, :].astype(F32)
            if parts > 1:
                zero = jnp.zeros((size, head_dim), F32)
                table[every(base + 3, size), :] = zero
                table[every(base + 4, size), :] = zero
            sums = cot_refs[m][n, size:, :].astype(F32)
            sums = sums[:lo_start] + sums[lo_start : 2 * lo_start]
            chosen = sums[:sum_rows]
            for r in range(1, rounds):
                chosen = jnp.where(hashing == r, sums[r * sum_rows : (r + 1) * sum_rows], chosen)
            log_sums[device, :sum_rows, :] = chosen
            return carry

        lax.fori_loop(0, chips, fill, 0)

    def gather(block):
        start = block * BLOCK

        def body(step, carry):
            for u in range(32):
                p = step * 32 + u
                row = pl.multiple_of(order[start + p] * TILE, TILE)
                picked[pl.ds(pl.multiple_of(p * TILE, TILE), TILE), :] = table[pl.ds(row, TILE), :]
            return carry

        lax.fori_loop(0, BLOCK // 32, body, 0)

    def scatter(block):
        start = block * BLOCK

        def body(step, carry):
            for u in range(32):
                p = step * 32 + u
                row = pl.multiple_of(order[start + p] * TILE, TILE)
                table[pl.ds(row, TILE), :] = packed[pl.ds(pl.multiple_of(p * TILE, TILE), TILE), :]
            return carry

        lax.fori_loop(0, BLOCK // 32, body, 0)

    def load(slot):
        q = picked[every(0, BLOCK), :]
        scale = lax.rsqrt(jnp.mean(q * q, axis=-1, keepdims=True) + EPS) * (1.0 / math.sqrt(head_dim))
        queries[slot] = q
        keys[slot] = (q * scale).astype(BF16)
        values[slot] = picked[every(1, BLOCK), :].astype(BF16)

    def finish(slot, block):
        q = queries[slot]
        d_key = dk[slot]
        scale = lax.rsqrt(jnp.mean(q * q, axis=-1, keepdims=True) + EPS)
        inner = jnp.mean(q * d_key, axis=-1, keepdims=True)
        pulled = (scale * (1.0 / math.sqrt(head_dim))) * (d_key - q * (scale * scale * inner))
        packed[every(3, BLOCK), :] = dq[slot] + pulled
        packed[every(4, BLOCK), :] = dv[slot]
        scatter(block)

    halo_block = lax.rem(first_block + block_total - 1, block_total)
    gather(halo_block)
    load(2)
    dk[2] = jnp.zeros_like(dk[2])
    dv[2] = jnp.zeros_like(dv[2])
    dq[2] = jnp.zeros_like(dq[2])

    row_id = lax.broadcasted_iota(jnp.int32, (BLOCK, BLOCK), 0)
    col_id = lax.broadcasted_iota(jnp.int32, (BLOCK, BLOCK), 1)
    diagonal = row_id == col_id

    def step(b, carry):
        block = first_block + b
        cur = lax.rem(b, 2)
        prev = jnp.where(b == 0, 2, 1 - cur)
        gather(block)
        load(cur)
        log_sum = jnp.concatenate(
            [log_sums[block, k : k + 1, :] for k in range(BLOCK // head_dim)], axis=1
        )
        cot = picked[every(2, BLOCK), :].astype(BF16)
        query = queries[cur].astype(BF16)
        key_a, key_b = keys[prev], keys[cur]
        w_a = jnp.exp(dot(key_a, query, NT) - log_sum)
        w_b = jnp.where(diagonal, 0.0, jnp.exp(dot(key_b, query, NT) - log_sum))
        dw_a = dot(values[prev], cot, NT)
        dw_b = dot(values[cur], cot, NT)
        delta = jnp.sum(w_a * dw_a + w_b * dw_b, axis=0, keepdims=True)
        ds_a = (w_a * (dw_a - delta)).astype(BF16)
        ds_b = (w_b * (dw_b - delta)).astype(BF16)
        dv[prev] = dv[prev] + dot(w_a.astype(BF16), cot, NN)
        dv[cur] = dot(w_b.astype(BF16), cot, NN)
        dk[prev] = dk[prev] + dot(ds_a, query, NN)
        dk[cur] = dot(ds_b, query, NN)
        dq[cur] = (dot(key_a, ds_a, TN) + dot(key_b, ds_b, TN)).T

        @pl.when(b > 0)
        def _():
            finish(prev, block - 1)

        return carry

    lax.fori_loop(0, blocks, step, 0)
    last = (blocks - 1) % 2
    if parts == 1:
        dk[last] = dk[last] + dk[2]
        dv[last] = dv[last] + dv[2]
    else:
        finish(2, halo_block)
    finish(last, first_block + blocks - 1)

    for m in range(per):

        def drain(n, carry):
            base = (n * per + ids[LANES, m]) * (size * TILE)
            out_refs[m][n, :, :head_dim] = table[every(base + 3, size), :].astype(BF16)
            out_refs[m][n, :, head_dim:] = table[every(base + 4, size), :].astype(BF16)
            return carry

        lax.fori_loop(0, chips, drain, 0)


def attention(per, parts, rounds, ids, order, qv, cot):
    chips = cot[0].shape[0]
    size, width = qv[0][0].shape[1:]
    head_dim = width // 2
    total = order.shape[0]
    blocks = total // BLOCK // parts
    smem = pl.BlockSpec(memory_space=pltpu.SMEM)
    vmem = pl.BlockSpec(memory_space=pltpu.VMEM)
    flat = [piece for lane in qv for piece in lane] + list(cot)
    return pl.pallas_call(
        partial(attention_kernel, per, parts, blocks, rounds, len(qv[0])),
        out_shape=[jax.ShapeDtypeStruct((chips, size, width), BF16)] * per,
        in_specs=[smem, smem] + [vmem] * len(flat),
        out_specs=[vmem] * per,
        scratch_shapes=[
            pltpu.VMEM((total * TILE, head_dim), F32),
            pltpu.VMEM((BLOCK * TILE, head_dim), F32),
            pltpu.VMEM((BLOCK * TILE, head_dim), F32),
            pltpu.VMEM((total // BLOCK, TILE, head_dim), F32),
            pltpu.VMEM((3, BLOCK, head_dim), BF16),
            pltpu.VMEM((3, BLOCK, head_dim), BF16),
            pltpu.VMEM((3, BLOCK, head_dim), F32),
            pltpu.VMEM((3, BLOCK, head_dim), F32),
            pltpu.VMEM((3, BLOCK, head_dim), F32),
            pltpu.VMEM((3, BLOCK, head_dim), F32),
        ],
        compiler_params=pltpu.CompilerParams(vmem_limit_bytes=VMEM_BYTES),
        name="attention",
    )(ids, order, *flat)


def prepare_kernel(tokens, gain, cot, log_sums, normal, chunks):
    heads, _, head_dim = chunks.shape
    size = tokens.shape[0]
    rounds = log_sums.shape[0]
    x = tokens[...].astype(F32)
    scale = lax.rsqrt(jnp.mean(x * x, axis=-1, keepdims=True) + EPS)
    normal[...] = (x * scale * gain[...]).astype(BF16)
    for h in range(heads):
        chunks[h, :size, :] = cot[:, h * head_dim : (h + 1) * head_dim]
        rows = [
            log_sums[r, h : h + 1, k * head_dim : (k + 1) * head_dim]
            for r in range(rounds)
            for k in range(size // head_dim)
        ]
        exact = jnp.concatenate(rows, axis=0)
        high = exact.astype(BF16).astype(F32)
        spare = jnp.zeros((chunks.shape[1] - size - 2 * len(rows), head_dim), F32)
        chunks[h, size:, :] = jnp.concatenate([high, exact - high, spare], axis=0).astype(BF16)


def prepare(tokens, gain, cot, log_sums):
    size, width = tokens.shape
    rounds, heads, _ = log_sums.shape
    head_dim = width // heads
    extra = 2 * rounds * size // head_dim
    extra = (extra + 15) // 16 * 16
    return pl.pallas_call(
        prepare_kernel,
        out_shape=[
            jax.ShapeDtypeStruct(tokens.shape, BF16),
            jax.ShapeDtypeStruct((heads, size + extra, head_dim), BF16),
        ],
        compiler_params=pltpu.CompilerParams(vmem_limit_bytes=SMALL_VMEM_BYTES),
        name="prepare",
    )(tokens, gain, cot, log_sums)


def weight_grad_kernel(per, count, ids, grads, *refs):
    shards = refs[:count]
    outs = refs[count : count + per]
    total = refs[count + per]
    chips, rows, _ = outs[0].shape
    grad_t = jnp.zeros((grads.shape[-1], shards[0].shape[-1]), F32)
    n = 0
    for shard in shards:
        grad_t = grad_t + dot(grads[ids[SHARDS, n]], shard[...], TN)
        n += 1
    total[...] = grad_t.T
    for m in range(per):
        for c in range(chips):
            start = pl.multiple_of((c * per + ids[LANES, m]) * rows, rows)
            outs[m][c] = total[pl.ds(start, rows), :].astype(BF16)


def weight_grad(per, rows, ids, grads, shards):
    chips, _, both = grads.shape
    smem = pl.BlockSpec(memory_space=pltpu.SMEM)
    vmem = pl.BlockSpec(memory_space=pltpu.VMEM)
    return pl.pallas_call(
        partial(weight_grad_kernel, per, len(shards)),
        out_shape=[jax.ShapeDtypeStruct((chips, rows, both), BF16)] * per,
        in_specs=[smem, vmem] + [vmem] * len(shards),
        out_specs=[vmem] * per,
        scratch_shapes=[pltpu.VMEM((shards[0].shape[1], both), F32)],
        compiler_params=pltpu.CompilerParams(vmem_limit_bytes=SMALL_VMEM_BYTES),
        name="weight_grad",
    )(ids, grads, *shards)


def home_kernel(scale_out, ids, grads, d_rows, w_qk, w_v, tokens, gain, out, d_wqk, d_wv, d_gain):
    heads, rows, both = d_rows.shape
    head_dim = both // 2
    total = jnp.zeros(tokens.shape, F32)
    start = pl.multiple_of(ids[LANES, ids.shape[1] - 1] * rows, rows)
    gains = jnp.zeros((rows, 1), F32)
    for head in range(heads):
        columns = slice(head * head_dim, (head + 1) * head_dim)
        weights = jnp.concatenate([w_qk[:, columns], w_v[:, columns]], axis=1)
        total = total + dot(grads[head], weights, NT)
        qk_rows = d_rows[head, :, :head_dim].astype(F32) * scale_out
        v_rows = d_rows[head, :, head_dim:].astype(F32) * scale_out
        d_wqk[:, columns] = qk_rows
        d_wv[:, columns] = v_rows
        own = qk_rows * w_qk[pl.ds(start, rows), columns].astype(F32)
        own = own + v_rows * w_v[pl.ds(start, rows), columns].astype(F32)
        gains = gains + jnp.sum(own, axis=1, keepdims=True)
    d_gain[...] = gains
    x = tokens[...].astype(F32)
    scale = lax.rsqrt(jnp.mean(x * x, axis=-1, keepdims=True) + EPS)
    scaled = total * gain[...]
    inner = jnp.mean(x * scaled, axis=-1, keepdims=True)
    out[...] = (scale * (scaled - x * (scale * scale * inner))).astype(BF16)


def home(scale_out, ids, grads, d_rows, w_qk, w_v, tokens, gain):
    rows = d_rows.shape[1]
    width = tokens.shape[1]
    smem = pl.BlockSpec(memory_space=pltpu.SMEM)
    vmem = pl.BlockSpec(memory_space=pltpu.VMEM)
    return pl.pallas_call(
        partial(home_kernel, scale_out),
        out_shape=[
            jax.ShapeDtypeStruct(tokens.shape, BF16),
            jax.ShapeDtypeStruct((rows, width), F32),
            jax.ShapeDtypeStruct((rows, width), F32),
            jax.ShapeDtypeStruct((rows, 1), F32),
        ],
        in_specs=[smem] + [vmem] * 6,
        out_specs=[vmem] * 4,
        compiler_params=pltpu.CompilerParams(vmem_limit_bytes=SMALL_VMEM_BYTES),
        name="home",
    )(ids, grads, d_rows, w_qk, w_v, tokens, gain)


def tables(devices, per, rounds, ring, block_total):
    chips = len(ring)
    place = [ring.index(c) for c in range(chips)]
    steps = [0]
    for s in range(1, chips // 2):
        steps += [-s, s]
    steps.append(chips // 2)
    out = np.zeros((devices, 2, max(chips, per + 3)), np.int32)
    for me in range(devices):
        chip, lane = me // per, me % per
        out[me, SHARDS, :chips] = [ring[(place[chip] + s) % chips] for s in steps]
        out[me, LANES, :per] = [(lane - m) % per for m in range(per)]
        out[me, LANES, per] = lane % rounds
        out[me, LANES, per + 1] = lane // rounds * (block_total * rounds // per)
        out[me, LANES, -1] = me
    return out


def per_device(tokens, norm_gain, w_qk, w_v, cotangent, log_sums, bucket_order, token_position):
    devices = lax.axis_size("tok")
    me = lax.axis_index("tok")
    size, width = tokens.shape
    rounds, heads, _ = log_sums.shape
    head_dim = width // heads
    total = bucket_order.shape[1]
    per = devices // heads
    parts = per // rounds
    chips = heads
    chip, lane = me // per, me % per
    groups = [[c * per + j for c in range(chips)] for j in range(per)]
    ring = list(range(0, chips, 2)) + list(range(chips - 1, 0, -2))

    def hop(x, distance):
        route = [
            (ring[p] * per + j, ring[(p + distance) % chips] * per + j)
            for p in range(chips)
            for j in range(per)
        ]
        return lax.ppermute(x, "tok", route)

    def swap(x, shift):
        route = [
            (c * per + j, c * per + (j + shift) % per) for c in range(chips) for j in range(per)
        ]
        return lax.ppermute(x, "tok", route)

    def exchange(x):
        return lax.all_to_all(x, "tok", 0, 0, tiled=True, axis_index_groups=groups)

    ids = lax.dynamic_index_in_dim(
        jnp.asarray(tables(devices, per, rounds, ring, total // BLOCK)), me, 0, keepdims=False
    )
    my_order = lax.dynamic_index_in_dim(bucket_order, lane % rounds, 0, keepdims=False)
    gain_row = norm_gain[None, :]
    normal, chunks = prepare(tokens, gain_row, cotangent, log_sums)

    shards = [normal]
    ahead = behind = normal
    half = chips // 2
    for s in range(1, half):
        ahead, behind = hop(ahead, 1), hop(behind, -1)
        shards += [ahead, behind]
    shards.append(
        jnp.concatenate([hop(ahead[: size // 2], 1), hop(behind[size // 2 :], -1)], axis=0)
    )
    cot = exchange(chunks)

    def my_columns(w):
        return lax.dynamic_slice_in_dim(w, chip * head_dim, head_dim, 1)

    my_weights = jnp.concatenate([my_columns(w_qk), my_columns(w_v)], axis=1)

    def project(some):
        return jnp.stack(
            [jnp.dot(n, my_weights, preferred_element_type=F32).astype(BF16) for n in some]
        )

    early = chips - 3
    qv = [project(shards[:early]), project(shards[early:])]
    qv_all = [qv] + [[swap(x, shift) for x in qv] for shift in range(1, per)]
    cot_all = [cot] + [swap(cot, shift) for shift in range(1, per)]
    sent = attention(per, parts, rounds, ids, my_order, qv_all, cot_all)
    grads = sent[0].astype(F32)
    for shift in range(1, per):
        grads = grads + swap(sent[shift], per - shift).astype(F32)
    grads = grads.astype(BF16)

    inbound = exchange(grads)
    rows = width // devices
    partials = weight_grad(per, rows, ids, grads, shards)
    mine = partials[0].astype(F32)
    for shift in range(1, per):
        mine = mine + swap(partials[shift], per - shift).astype(F32)
    d_rows = exchange(mine.astype(BF16))
    d_tokens, d_wqk, d_wv, gains = home(
        1.0 / math.sqrt(total), ids, inbound, d_rows, w_qk, w_v, tokens, gain_row
    )
    d_gain = gains[:, 0] / lax.dynamic_slice_in_dim(norm_gain, me * rows, rows, 0)
    return d_tokens, d_gain, d_wqk, d_wv


def solution(mesh):
    in_specs = (
        P(("groups", "tok"), None),
        P(),
        P(),
        P(),
        P(("groups", "tok"), None),
        P(None, None, ("groups", "tok")),
        P(None, "groups"),
        P(None, ("groups", "tok")),
    )
    out_specs = (
        P(("groups", "tok"), None),
        P(("groups", "tok")),
        P(("groups", "tok"), None),
        P(("groups", "tok"), None),
    )
    return jax.shard_map(
        per_device, mesh=mesh, in_specs=in_specs, out_specs=out_specs, check_vma=False
    )
```

```python
import math
from functools import partial

import jax
import jax.numpy as jnp
import numpy as np
from jax import lax
from jax.experimental import pallas as pl
from jax.experimental.pallas import tpu as pltpu
from jax.sharding import PartitionSpec as P

BLOCK = 256
EPS = 1e-06
F32 = jnp.float32
BF16 = jnp.bfloat16
TILE = 8
NN = (((1,), (0,)), ((), ()))
NT = (((1,), (1,)), ((), ()))
TN = (((0,), (0,)), ((), ()))
VMEM_BYTES = 60 * 1024 * 1024
SMALL_VMEM_BYTES = 24 * 1024 * 1024
SHARDS, LANES = 0, 1


def dot(a, b, dims):
    return lax.dot_general(a, b, dims, preferred_element_type=F32)


def every(lead, size):
    return pl.ds(lead, size, stride=TILE)


def attention_kernel(per, parts, blocks, rounds, pieces, ids, order, *refs):
    qv_refs = [refs[m * pieces : (m + 1) * pieces] for m in range(per)]
    refs = refs[per * pieces :]
    cot_refs = refs[:per]
    out_refs = refs[per : 2 * per]
    table, picked, packed, log_sums, keys, values, queries, dq, dk, dv = refs[2 * per :]
    chips, size, width = out_refs[0].shape
    head_dim = width // 2
    total = table.shape[0] // TILE
    block_total = total // BLOCK
    sum_rows = size // head_dim
    lo_start = rounds * sum_rows
    hashing = ids[LANES, per]
    first_block = ids[LANES, per + 1]

    for m in range(per):
        n = 0
        for ref in qv_refs[m]:
            for row in range(ref.shape[0]):
                base = (ids[SHARDS, n] * per + ids[LANES, m]) * (size * TILE)
                table[every(base, size), :] = ref[row, :, :head_dim].astype(F32)
                table[every(base + 1, size), :] = ref[row, :, head_dim:].astype(F32)
                n += 1

        def fill(n, carry):
            device = n * per + ids[LANES, m]
            base = device * (size * TILE)
            table[every(base + 2, size), :] = cot_refs[m][n, :size, :].astype(F32)
            if parts > 1:
                zero = jnp.zeros((size, head_dim), F32)
                table[every(base + 3, size), :] = zero
                table[every(base + 4, size), :] = zero
            sums = cot_refs[m][n, size:, :].astype(F32)
            sums = sums[:lo_start] + sums[lo_start : 2 * lo_start]
            chosen = sums[:sum_rows]
            for r in range(1, rounds):
                chosen = jnp.where(hashing == r, sums[r * sum_rows : (r + 1) * sum_rows], chosen)
            log_sums[device, :sum_rows, :] = chosen
            return carry

        lax.fori_loop(0, chips, fill, 0)

    def gather(block):
        start = block * BLOCK

        def body(step, carry):
            for u in range(32):
                p = step * 32 + u
                row = pl.multiple_of(order[start + p] * TILE, TILE)
                picked[pl.ds(pl.multiple_of(p * TILE, TILE), TILE), :] = table[pl.ds(row, TILE), :]
            return carry

        lax.fori_loop(0, BLOCK // 32, body, 0)

    def scatter(block):
        start = block * BLOCK

        def body(step, carry):
            for u in range(32):
                p = step * 32 + u
                row = pl.multiple_of(order[start + p] * TILE, TILE)
                table[pl.ds(row, TILE), :] = packed[pl.ds(pl.multiple_of(p * TILE, TILE), TILE), :]
            return carry

        lax.fori_loop(0, BLOCK // 32, body, 0)

    def load(slot):
        q = picked[every(0, BLOCK), :]
        scale = lax.rsqrt(jnp.mean(q * q, axis=-1, keepdims=True) + EPS) * (1.0 / math.sqrt(head_dim))
        queries[slot] = q
        keys[slot] = (q * scale).astype(BF16)
        values[slot] = picked[every(1, BLOCK), :].astype(BF16)

    def finish(slot, block):
        q = queries[slot]
        d_key = dk[slot]
        scale = lax.rsqrt(jnp.mean(q * q, axis=-1, keepdims=True) + EPS)
        inner = jnp.mean(q * d_key, axis=-1, keepdims=True)
        pulled = (scale * (1.0 / math.sqrt(head_dim))) * (d_key - q * (scale * scale * inner))
        packed[every(3, BLOCK), :] = dq[slot] + pulled
        packed[every(4, BLOCK), :] = dv[slot]
        scatter(block)

    halo_block = lax.rem(first_block + block_total - 1, block_total)
    gather(halo_block)
    load(2)
    dk[2] = jnp.zeros_like(dk[2])
    dv[2] = jnp.zeros_like(dv[2])
    dq[2] = jnp.zeros_like(dq[2])

    row_id = lax.broadcasted_iota(jnp.int32, (BLOCK, BLOCK), 0)
    col_id = lax.broadcasted_iota(jnp.int32, (BLOCK, BLOCK), 1)
    diagonal = row_id == col_id

    def step(b, carry):
        block = first_block + b
        cur = lax.rem(b, 2)
        prev = jnp.where(b == 0, 2, 1 - cur)
        gather(block)
        load(cur)
        log_sum = jnp.concatenate(
            [log_sums[block, k : k + 1, :] for k in range(BLOCK // head_dim)], axis=1
        )
        cot = picked[every(2, BLOCK), :].astype(BF16)
        query = queries[cur].astype(BF16)
        key_a, key_b = keys[prev], keys[cur]
        w_a = jnp.exp(dot(key_a, query, NT) - log_sum)
        w_b = jnp.where(diagonal, 0.0, jnp.exp(dot(key_b, query, NT) - log_sum))
        dw_a = dot(values[prev], cot, NT)
        dw_b = dot(values[cur], cot, NT)
        delta = jnp.sum(w_a * dw_a + w_b * dw_b, axis=0, keepdims=True)
        ds_a = (w_a * (dw_a - delta)).astype(BF16)
        ds_b = (w_b * (dw_b - delta)).astype(BF16)
        dv[prev] = dv[prev] + dot(w_a.astype(BF16), cot, NN)
        dv[cur] = dot(w_b.astype(BF16), cot, NN)
        dk[prev] = dk[prev] + dot(ds_a, query, NN)
        dk[cur] = dot(ds_b, query, NN)
        dq[cur] = (dot(key_a, ds_a, TN) + dot(key_b, ds_b, TN)).T

        @pl.when(b > 0)
        def _():
            finish(prev, block - 1)

        return carry

    lax.fori_loop(0, blocks, step, 0)
    last = (blocks - 1) % 2
    if parts == 1:
        dk[last] = dk[last] + dk[2]
        dv[last] = dv[last] + dv[2]
    else:
        finish(2, halo_block)
    finish(last, first_block + blocks - 1)

    for m in range(per):

        def drain(n, carry):
            base = (n * per + ids[LANES, m]) * (size * TILE)
            out_refs[m][n, :, :head_dim] = table[every(base + 3, size), :].astype(BF16)
            out_refs[m][n, :, head_dim:] = table[every(base + 4, size), :].astype(BF16)
            return carry

        lax.fori_loop(0, chips, drain, 0)


def attention(per, parts, rounds, ids, order, qv, cot):
    chips = cot[0].shape[0]
    size, width = qv[0][0].shape[1:]
    head_dim = width // 2
    total = order.shape[0]
    blocks = total // BLOCK // parts
    smem = pl.BlockSpec(memory_space=pltpu.SMEM)
    vmem = pl.BlockSpec(memory_space=pltpu.VMEM)
    flat = [piece for lane in qv for piece in lane] + list(cot)
    return pl.pallas_call(
        partial(attention_kernel, per, parts, blocks, rounds, len(qv[0])),
        out_shape=[jax.ShapeDtypeStruct((chips, size, width), BF16)] * per,
        in_specs=[smem, smem] + [vmem] * len(flat),
        out_specs=[vmem] * per,
        scratch_shapes=[
            pltpu.VMEM((total * TILE, head_dim), F32),
            pltpu.VMEM((BLOCK * TILE, head_dim), F32),
            pltpu.VMEM((BLOCK * TILE, head_dim), F32),
            pltpu.VMEM((total // BLOCK, TILE, head_dim), F32),
            pltpu.VMEM((3, BLOCK, head_dim), BF16),
            pltpu.VMEM((3, BLOCK, head_dim), BF16),
            pltpu.VMEM((3, BLOCK, head_dim), F32),
            pltpu.VMEM((3, BLOCK, head_dim), F32),
            pltpu.VMEM((3, BLOCK, head_dim), F32),
            pltpu.VMEM((3, BLOCK, head_dim), F32),
        ],
        compiler_params=pltpu.CompilerParams(vmem_limit_bytes=VMEM_BYTES),
        name="attention",
    )(ids, order, *flat)


def prepare_kernel(tokens, gain, cot, log_sums, normal, chunks):
    heads, _, head_dim = chunks.shape
    size = tokens.shape[0]
    rounds = log_sums.shape[0]
    x = tokens[...].astype(F32)
    scale = lax.rsqrt(jnp.mean(x * x, axis=-1, keepdims=True) + EPS)
    normal[...] = (x * scale * gain[...]).astype(BF16)
    for h in range(heads):
        chunks[h, :size, :] = cot[:, h * head_dim : (h + 1) * head_dim]
        rows = [
            log_sums[r, h : h + 1, k * head_dim : (k + 1) * head_dim]
            for r in range(rounds)
            for k in range(size // head_dim)
        ]
        exact = jnp.concatenate(rows, axis=0)
        high = exact.astype(BF16).astype(F32)
        spare = jnp.zeros((chunks.shape[1] - size - 2 * len(rows), head_dim), F32)
        chunks[h, size:, :] = jnp.concatenate([high, exact - high, spare], axis=0).astype(BF16)


def prepare(tokens, gain, cot, log_sums):
    size, width = tokens.shape
    rounds, heads, _ = log_sums.shape
    head_dim = width // heads
    extra = 2 * rounds * size // head_dim
    extra = (extra + 15) // 16 * 16
    return pl.pallas_call(
        prepare_kernel,
        out_shape=[
            jax.ShapeDtypeStruct(tokens.shape, BF16),
            jax.ShapeDtypeStruct((heads, size + extra, head_dim), BF16),
        ],
        compiler_params=pltpu.CompilerParams(vmem_limit_bytes=SMALL_VMEM_BYTES),
        name="prepare",
    )(tokens, gain, cot, log_sums)


def weight_grad_kernel(per, count, ids, grads, *refs):
    shards = refs[:count]
    outs = refs[count : count + per]
    total = refs[count + per]
    chips, rows, _ = outs[0].shape
    grad_t = jnp.zeros((grads.shape[-1], shards[0].shape[-1]), F32)
    n = 0
    for shard in shards:
        grad_t = grad_t + dot(grads[ids[SHARDS, n]], shard[...], TN)
        n += 1
    total[...] = grad_t.T
    for m in range(per):
        for k in range(chips):
            chip = lax.rem(ids[SHARDS, 0] + k, chips)
            start = pl.multiple_of((chip * per + ids[LANES, m]) * rows, rows)
            outs[m][k] = total[pl.ds(start, rows), :].astype(BF16)


def weight_grad(per, rows, ids, grads, shards):
    chips, _, both = grads.shape
    smem = pl.BlockSpec(memory_space=pltpu.SMEM)
    vmem = pl.BlockSpec(memory_space=pltpu.VMEM)
    return pl.pallas_call(
        partial(weight_grad_kernel, per, len(shards)),
        out_shape=[jax.ShapeDtypeStruct((chips, rows, both), BF16)] * per,
        in_specs=[smem, vmem] + [vmem] * len(shards),
        out_specs=[vmem] * per,
        scratch_shapes=[pltpu.VMEM((shards[0].shape[1], both), F32)],
        compiler_params=pltpu.CompilerParams(vmem_limit_bytes=SMALL_VMEM_BYTES),
        name="weight_grad",
    )(ids, grads, *shards)


def home_kernel(scale_out, ids, grads, w_qk, w_v, tokens, gain, *refs):
    heads = grads.shape[0]
    d_rows = refs[:heads]
    out, d_wqk, d_wv, d_gain = refs[heads:]
    rows, both = d_rows[0].shape
    head_dim = both // 2
    total = jnp.zeros(tokens.shape, F32)
    start = pl.multiple_of(ids[LANES, ids.shape[1] - 1] * rows, rows)
    gains = jnp.zeros((rows, 1), F32)
    for head in range(heads):
        columns = slice(head * head_dim, (head + 1) * head_dim)
        weights = jnp.concatenate([w_qk[:, columns], w_v[:, columns]], axis=1)
        total = total + dot(grads[head], weights, NT)
        k = head
        source = lax.rem(ids[SHARDS, 0] + heads - k, heads)
        columns = pl.ds(pl.multiple_of(source * head_dim, head_dim), head_dim)
        qk_rows = d_rows[k][:, :head_dim].astype(F32) * scale_out
        v_rows = d_rows[k][:, head_dim:].astype(F32) * scale_out
        d_wqk[:, columns] = qk_rows
        d_wv[:, columns] = v_rows
        own = qk_rows * w_qk[pl.ds(start, rows), columns].astype(F32)
        own = own + v_rows * w_v[pl.ds(start, rows), columns].astype(F32)
        gains = gains + jnp.sum(own, axis=1, keepdims=True)
    d_gain[...] = gains
    x = tokens[...].astype(F32)
    scale = lax.rsqrt(jnp.mean(x * x, axis=-1, keepdims=True) + EPS)
    scaled = total * gain[...]
    inner = jnp.mean(x * scaled, axis=-1, keepdims=True)
    out[...] = (scale * (scaled - x * (scale * scale * inner))).astype(BF16)


def home(scale_out, ids, grads, d_rows, w_qk, w_v, tokens, gain):
    rows = d_rows[0].shape[0]
    width = tokens.shape[1]
    smem = pl.BlockSpec(memory_space=pltpu.SMEM)
    vmem = pl.BlockSpec(memory_space=pltpu.VMEM)
    return pl.pallas_call(
        partial(home_kernel, scale_out),
        out_shape=[
            jax.ShapeDtypeStruct(tokens.shape, BF16),
            jax.ShapeDtypeStruct((rows, width), F32),
            jax.ShapeDtypeStruct((rows, width), F32),
            jax.ShapeDtypeStruct((rows, 1), F32),
        ],
        in_specs=[smem] + [vmem] * (5 + len(d_rows)),
        out_specs=[vmem] * 4,
        compiler_params=pltpu.CompilerParams(vmem_limit_bytes=SMALL_VMEM_BYTES),
        name="home",
    )(ids, grads, w_qk, w_v, tokens, gain, *d_rows)


def tables(devices, per, rounds, ring, block_total):
    chips = len(ring)
    place = [ring.index(c) for c in range(chips)]
    steps = [0]
    for s in range(1, chips // 2):
        steps += [-s, s]
    steps.append(chips // 2)
    out = np.zeros((devices, 2, max(chips, per + 3)), np.int32)
    for me in range(devices):
        chip, lane = me // per, me % per
        out[me, SHARDS, :chips] = [ring[(place[chip] + s) % chips] for s in steps]
        out[me, LANES, :per] = [(lane - m) % per for m in range(per)]
        out[me, LANES, per] = lane % rounds
        out[me, LANES, per + 1] = lane // rounds * (block_total * rounds // per)
        out[me, LANES, -1] = me
    return out


def per_device(tokens, norm_gain, w_qk, w_v, cotangent, log_sums, bucket_order, token_position):
    devices = lax.axis_size("tok")
    me = lax.axis_index("tok")
    size, width = tokens.shape
    rounds, heads, _ = log_sums.shape
    head_dim = width // heads
    total = bucket_order.shape[1]
    per = devices // heads
    parts = per // rounds
    chips = heads
    chip, lane = me // per, me % per
    groups = [[c * per + j for c in range(chips)] for j in range(per)]
    ring = list(range(0, chips, 2)) + list(range(chips - 1, 0, -2))

    def hop(x, distance):
        route = [
            (ring[p] * per + j, ring[(p + distance) % chips] * per + j)
            for p in range(chips)
            for j in range(per)
        ]
        return lax.ppermute(x, "tok", route)

    def swap(x, shift):
        route = [
            (c * per + j, c * per + (j + shift) % per) for c in range(chips) for j in range(per)
        ]
        return lax.ppermute(x, "tok", route)

    def send(x, distance):
        route = [
            (c * per + j, (c + distance) % chips * per + j) for c in range(chips) for j in range(per)
        ]
        return lax.ppermute(x, "tok", route)

    def exchange(x):
        return lax.all_to_all(x, "tok", 0, 0, tiled=True, axis_index_groups=groups)

    ids = lax.dynamic_index_in_dim(
        jnp.asarray(tables(devices, per, rounds, ring, total // BLOCK)), me, 0, keepdims=False
    )
    my_order = lax.dynamic_index_in_dim(bucket_order, lane % rounds, 0, keepdims=False)
    gain_row = norm_gain[None, :]
    normal, chunks = prepare(tokens, gain_row, cotangent, log_sums)

    shards = [normal]
    ahead = behind = normal
    half = chips // 2
    for s in range(1, half):
        ahead, behind = hop(ahead, 1), hop(behind, -1)
        shards += [ahead, behind]
    shards.append(
        jnp.concatenate([hop(ahead[: size // 2], 1), hop(behind[size // 2 :], -1)], axis=0)
    )
    cot = exchange(chunks)

    def my_columns(w):
        return lax.dynamic_slice_in_dim(w, chip * head_dim, head_dim, 1)

    my_weights = jnp.concatenate([my_columns(w_qk), my_columns(w_v)], axis=1)

    def project(some):
        return jnp.stack(
            [jnp.dot(n, my_weights, preferred_element_type=F32).astype(BF16) for n in some]
        )

    early = chips - 3
    qv = [project(shards[:early]), project(shards[early:])]
    qv_all = [qv] + [[swap(x, shift) for x in qv] for shift in range(1, per)]
    cot_all = [cot] + [swap(cot, shift) for shift in range(1, per)]
    sent = attention(per, parts, rounds, ids, my_order, qv_all, cot_all)
    grads = sent[0].astype(F32)
    for shift in range(1, per):
        grads = grads + swap(sent[shift], per - shift).astype(F32)
    grads = grads.astype(BF16)

    inbound = exchange(grads)
    rows = width // devices
    partials = weight_grad(per, rows, ids, grads, shards)
    mine = partials[0].astype(F32)
    for shift in range(1, per):
        mine = mine + swap(partials[shift], per - shift).astype(F32)
    mine = mine.astype(BF16)
    d_rows = [mine[0]] + [send(mine[k], k) for k in range(1, chips)]
    d_tokens, d_wqk, d_wv, gains = home(
        1.0 / math.sqrt(total), ids, inbound, d_rows, w_qk, w_v, tokens, gain_row
    )
    d_gain = gains[:, 0] / lax.dynamic_slice_in_dim(norm_gain, me * rows, rows, 0)
    return d_tokens, d_gain, d_wqk, d_wv


def solution(mesh):
    in_specs = (
        P(("groups", "tok"), None),
        P(),
        P(),
        P(),
        P(("groups", "tok"), None),
        P(None, None, ("groups", "tok")),
        P(None, "groups"),
        P(None, ("groups", "tok")),
    )
    out_specs = (
        P(("groups", "tok"), None),
        P(("groups", "tok")),
        P(("groups", "tok"), None),
        P(("groups", "tok"), None),
    )
    return jax.shard_map(
        per_device, mesh=mesh, in_specs=in_specs, out_specs=out_specs, check_vma=False
    )
```

```python
import math
from functools import partial

import jax
import jax.numpy as jnp
import numpy as np
from jax import lax
from jax.experimental import pallas as pl
from jax.experimental.pallas import tpu as pltpu
from jax.sharding import PartitionSpec as P

BLOCK = 256
EPS = 1e-06
F32 = jnp.float32
BF16 = jnp.bfloat16
TILE = 8
NN = (((1,), (0,)), ((), ()))
NT = (((1,), (1,)), ((), ()))
TN = (((0,), (0,)), ((), ()))
VMEM_BYTES = 60 * 1024 * 1024
SMALL_VMEM_BYTES = 24 * 1024 * 1024
SHARDS, LANES = 0, 1


def dot(a, b, dims):
    return lax.dot_general(a, b, dims, preferred_element_type=F32)


def every(lead, size):
    return pl.ds(lead, size, stride=TILE)


def attention_kernel(per, parts, blocks, rounds, pieces, ids, order, *refs):
    qv_refs = [refs[m * pieces : (m + 1) * pieces] for m in range(per)]
    refs = refs[per * pieces :]
    cot_refs = refs[:per]
    out_refs = refs[per : 2 * per]
    table, picked, packed, log_sums, keys, values, queries, dq, dk, dv, halo = refs[2 * per :]
    chips, size, width = out_refs[0].shape
    head_dim = width // 2
    total = table.shape[0] // TILE
    block_total = total // BLOCK
    sum_rows = size // head_dim
    lo_start = rounds * sum_rows
    hashing = ids[LANES, per]
    first_block = ids[LANES, per + 1]

    for m in range(per):
        n = 0
        for ref in qv_refs[m]:
            for row in range(ref.shape[0]):
                base = (ids[SHARDS, n] * per + ids[LANES, m]) * (size * TILE)
                table[every(base, size), :] = ref[row, :, :head_dim].astype(F32)
                table[every(base + 1, size), :] = ref[row, :, head_dim:].astype(F32)
                n += 1

        def fill(n, carry):
            device = n * per + ids[LANES, m]
            base = device * (size * TILE)
            table[every(base + 2, size), :] = cot_refs[m][n, :size, :].astype(F32)
            if parts > 1:
                zero = jnp.zeros((size, head_dim), F32)
                table[every(base + 3, size), :] = zero
                table[every(base + 4, size), :] = zero
            sums = cot_refs[m][n, size:, :].astype(F32)
            sums = sums[:lo_start] + sums[lo_start : 2 * lo_start]
            chosen = sums[:sum_rows]
            for r in range(1, rounds):
                chosen = jnp.where(hashing == r, sums[r * sum_rows : (r + 1) * sum_rows], chosen)
            log_sums[device, :sum_rows, :] = chosen
            return carry

        lax.fori_loop(0, chips, fill, 0)

    def rows_of(block):
        start = lax.rem(block, block_total) * BLOCK
        for p in range(BLOCK):
            yield p * TILE, pl.multiple_of(order[start + p] * TILE, TILE)

    def gather(block, slot):
        for place, row in rows_of(block):
            picked[slot, place : place + TILE, :] = table[pl.ds(row, TILE), :]

    def scatter(block, slot):
        for place, row in rows_of(block):
            table[pl.ds(row, TILE), :] = packed[slot, place : place + TILE, :]

    def load(slot):
        q = picked[slot, every(0, BLOCK), :]
        scale = lax.rsqrt(jnp.mean(q * q, axis=-1, keepdims=True) + EPS) * (1.0 / math.sqrt(head_dim))
        queries[slot] = q
        keys[slot] = (q * scale).astype(BF16)
        values[slot] = picked[slot, every(1, BLOCK), :].astype(BF16)

    def finish(slot, q, d_query, d_key, d_value):
        scale = lax.rsqrt(jnp.mean(q * q, axis=-1, keepdims=True) + EPS)
        inner = jnp.mean(q * d_key, axis=-1, keepdims=True)
        pulled = (scale * (1.0 / math.sqrt(head_dim))) * (d_key - q * (scale * scale * inner))
        packed[slot, every(3, BLOCK), :] = pulled if d_query is None else d_query + pulled
        packed[slot, every(4, BLOCK), :] = d_value

    diagonal = lax.broadcasted_iota(jnp.int32, (BLOCK, BLOCK), 0) == lax.broadcasted_iota(
        jnp.int32, (BLOCK, BLOCK), 1
    )

    def step(b, cur, first=False, write=True):
        block = first_block + b
        prev = 1 - cur
        gather(block + 1, prev)
        if write:
            scatter(block - 2, cur)
        load(cur)
        log_sum = jnp.concatenate(
            [log_sums[block, k : k + 1, :] for k in range(BLOCK // head_dim)], axis=1
        )
        cot = picked[cur, every(2, BLOCK), :].astype(BF16)
        query = queries[cur].astype(BF16)
        key_a, key_b = keys[prev], keys[cur]
        w_a = jnp.exp(dot(key_a, query, NT) - log_sum)
        w_b = jnp.where(diagonal, 0.0, jnp.exp(dot(key_b, query, NT) - log_sum))
        dw_a = dot(values[prev], cot, NT)
        dw_b = dot(values[cur], cot, NT)
        delta = jnp.sum(w_a * dw_a + w_b * dw_b, axis=0, keepdims=True)
        ds_a = (w_a * (dw_a - delta)).astype(BF16)
        ds_b = (w_b * (dw_b - delta)).astype(BF16)
        dv_a = dot(w_a.astype(BF16), cot, NN)
        dk_a = dot(ds_a, query, NN)
        if first:
            halo[0] = dk_a
            halo[1] = dv_a
        else:
            finish(prev, queries[prev], dq[prev], dk[prev] + dk_a, dv[prev] + dv_a)
        dv[cur] = dot(w_b.astype(BF16), cot, NN)
        dk[cur] = dot(ds_b, query, NN)
        dq[cur] = (dot(key_a, ds_a, TN) + dot(key_b, ds_b, TN)).T

    halo_block = first_block + block_total - 1
    gather(halo_block, 1)
    load(1)
    if parts > 1:
        halo[2] = queries[1]
    gather(first_block, 0)
    step(0, 0, first=True, write=False)
    step(1, 1, write=False)

    def pair(i, carry):
        step(2 * i, 0)
        step(2 * i + 1, 1)
        return carry

    lax.fori_loop(1, blocks // 2, pair, 0)
    if blocks % 2:
        step(blocks - 1, 0)
    last = (blocks - 1) % 2
    scatter(first_block + blocks - 2, 1 - last)
    if parts == 1:
        finish(last, queries[last], dq[last], dk[last] + halo[0], dv[last] + halo[1])
    else:
        finish(1 - last, halo[2], None, halo[0], halo[1])
        scatter(halo_block, 1 - last)
        finish(last, queries[last], dq[last], dk[last], dv[last])
    scatter(first_block + blocks - 1, last)

    for m in range(per):

        def drain(n, carry):
            base = (n * per + ids[LANES, m]) * (size * TILE)
            out_refs[m][n, :, :head_dim] = table[every(base + 3, size), :].astype(BF16)
            out_refs[m][n, :, head_dim:] = table[every(base + 4, size), :].astype(BF16)
            return carry

        lax.fori_loop(0, chips, drain, 0)


def attention(per, parts, rounds, ids, order, qv, cot):
    chips = cot[0].shape[0]
    size, width = qv[0][0].shape[1:]
    head_dim = width // 2
    total = order.shape[0]
    blocks = total // BLOCK // parts
    smem = pl.BlockSpec(memory_space=pltpu.SMEM)
    vmem = pl.BlockSpec(memory_space=pltpu.VMEM)
    flat = [piece for lane in qv for piece in lane] + list(cot)
    return pl.pallas_call(
        partial(attention_kernel, per, parts, blocks, rounds, len(qv[0])),
        out_shape=[jax.ShapeDtypeStruct((chips, size, width), BF16)] * per,
        in_specs=[smem, smem] + [vmem] * len(flat),
        out_specs=[vmem] * per,
        scratch_shapes=[
            pltpu.VMEM((total * TILE, head_dim), F32),
            pltpu.VMEM((2, BLOCK * TILE, head_dim), F32),
            pltpu.VMEM((2, BLOCK * TILE, head_dim), F32),
            pltpu.VMEM((total // BLOCK, TILE, head_dim), F32),
            pltpu.VMEM((2, BLOCK, head_dim), BF16),
            pltpu.VMEM((2, BLOCK, head_dim), BF16),
            pltpu.VMEM((2, BLOCK, head_dim), F32),
            pltpu.VMEM((2, BLOCK, head_dim), F32),
            pltpu.VMEM((2, BLOCK, head_dim), F32),
            pltpu.VMEM((2, BLOCK, head_dim), F32),
            pltpu.VMEM((3, BLOCK, head_dim), F32),
        ],
        compiler_params=pltpu.CompilerParams(vmem_limit_bytes=VMEM_BYTES),
        name="attention",
    )(ids, order, *flat)


def prepare_kernel(tokens, gain, cot, log_sums, normal, chunks):
    heads, _, head_dim = chunks.shape
    size = tokens.shape[0]
    rounds = log_sums.shape[0]
    x = tokens[...].astype(F32)
    scale = lax.rsqrt(jnp.mean(x * x, axis=-1, keepdims=True) + EPS)
    normal[...] = (x * scale * gain[...]).astype(BF16)
    for h in range(heads):
        chunks[h, :size, :] = cot[:, h * head_dim : (h + 1) * head_dim]
        rows = [
            log_sums[r, h : h + 1, k * head_dim : (k + 1) * head_dim]
            for r in range(rounds)
            for k in range(size // head_dim)
        ]
        exact = jnp.concatenate(rows, axis=0)
        high = exact.astype(BF16).astype(F32)
        spare = jnp.zeros((chunks.shape[1] - size - 2 * len(rows), head_dim), F32)
        chunks[h, size:, :] = jnp.concatenate([high, exact - high, spare], axis=0).astype(BF16)


def prepare(tokens, gain, cot, log_sums):
    size, width = tokens.shape
    rounds, heads, _ = log_sums.shape
    head_dim = width // heads
    extra = 2 * rounds * size // head_dim
    extra = (extra + 15) // 16 * 16
    return pl.pallas_call(
        prepare_kernel,
        out_shape=[
            jax.ShapeDtypeStruct(tokens.shape, BF16),
            jax.ShapeDtypeStruct((heads, size + extra, head_dim), BF16),
        ],
        compiler_params=pltpu.CompilerParams(vmem_limit_bytes=SMALL_VMEM_BYTES),
        name="prepare",
    )(tokens, gain, cot, log_sums)


def weight_grad_kernel(per, count, ids, grads, *refs):
    shards = refs[:count]
    outs = refs[count : count + per]
    total = refs[count + per]
    chips, rows, _ = outs[0].shape
    grad_t = jnp.zeros((grads.shape[-1], shards[0].shape[-1]), F32)
    n = 0
    for shard in shards:
        grad_t = grad_t + dot(grads[ids[SHARDS, n]], shard[...], TN)
        n += 1
    total[...] = grad_t.T
    for m in range(per):
        for k in range(chips):
            chip = lax.rem(ids[SHARDS, 0] + k, chips)
            start = pl.multiple_of((chip * per + ids[LANES, m]) * rows, rows)
            outs[m][k] = total[pl.ds(start, rows), :].astype(BF16)


def weight_grad(per, rows, ids, grads, shards):
    chips, _, both = grads.shape
    smem = pl.BlockSpec(memory_space=pltpu.SMEM)
    vmem = pl.BlockSpec(memory_space=pltpu.VMEM)
    return pl.pallas_call(
        partial(weight_grad_kernel, per, len(shards)),
        out_shape=[jax.ShapeDtypeStruct((chips, rows, both), BF16)] * per,
        in_specs=[smem, vmem] + [vmem] * len(shards),
        out_specs=[vmem] * per,
        scratch_shapes=[pltpu.VMEM((shards[0].shape[1], both), F32)],
        compiler_params=pltpu.CompilerParams(vmem_limit_bytes=SMALL_VMEM_BYTES),
        name="weight_grad",
    )(ids, grads, *shards)


def home_kernel(scale_out, ids, grads, w_qk, w_v, tokens, gain, *refs):
    heads = grads.shape[0]
    d_rows = refs[:heads]
    out, d_wqk, d_wv, d_gain = refs[heads:]
    rows, both = d_rows[0].shape
    head_dim = both // 2
    total = jnp.zeros(tokens.shape, F32)
    start = pl.multiple_of(ids[LANES, ids.shape[1] - 1] * rows, rows)
    gains = jnp.zeros((rows, 1), F32)
    for head in range(heads):
        columns = slice(head * head_dim, (head + 1) * head_dim)
        weights = jnp.concatenate([w_qk[:, columns], w_v[:, columns]], axis=1)
        total = total + dot(grads[head], weights, NT)
        k = head
        source = lax.rem(ids[SHARDS, 0] + heads - k, heads)
        columns = pl.ds(pl.multiple_of(source * head_dim, head_dim), head_dim)
        qk_rows = d_rows[k][:, :head_dim].astype(F32) * scale_out
        v_rows = d_rows[k][:, head_dim:].astype(F32) * scale_out
        d_wqk[:, columns] = qk_rows
        d_wv[:, columns] = v_rows
        own = qk_rows * w_qk[pl.ds(start, rows), columns].astype(F32)
        own = own + v_rows * w_v[pl.ds(start, rows), columns].astype(F32)
        gains = gains + jnp.sum(own, axis=1, keepdims=True)
    d_gain[...] = gains
    x = tokens[...].astype(F32)
    scale = lax.rsqrt(jnp.mean(x * x, axis=-1, keepdims=True) + EPS)
    scaled = total * gain[...]
    inner = jnp.mean(x * scaled, axis=-1, keepdims=True)
    out[...] = (scale * (scaled - x * (scale * scale * inner))).astype(BF16)


def home(scale_out, ids, grads, d_rows, w_qk, w_v, tokens, gain):
    rows = d_rows[0].shape[0]
    width = tokens.shape[1]
    smem = pl.BlockSpec(memory_space=pltpu.SMEM)
    vmem = pl.BlockSpec(memory_space=pltpu.VMEM)
    return pl.pallas_call(
        partial(home_kernel, scale_out),
        out_shape=[
            jax.ShapeDtypeStruct(tokens.shape, BF16),
            jax.ShapeDtypeStruct((rows, width), F32),
            jax.ShapeDtypeStruct((rows, width), F32),
            jax.ShapeDtypeStruct((rows, 1), F32),
        ],
        in_specs=[smem] + [vmem] * (5 + len(d_rows)),
        out_specs=[vmem] * 4,
        compiler_params=pltpu.CompilerParams(vmem_limit_bytes=SMALL_VMEM_BYTES),
        name="home",
    )(ids, grads, w_qk, w_v, tokens, gain, *d_rows)


def tables(devices, per, rounds, ring, block_total):
    chips = len(ring)
    place = [ring.index(c) for c in range(chips)]
    steps = [0]
    for s in range(1, chips // 2):
        steps += [-s, s]
    steps.append(chips // 2)
    out = np.zeros((devices, 2, max(chips, per + 3)), np.int32)
    for me in range(devices):
        chip, lane = me // per, me % per
        out[me, SHARDS, :chips] = [ring[(place[chip] + s) % chips] for s in steps]
        out[me, LANES, :per] = [(lane - m) % per for m in range(per)]
        out[me, LANES, per] = lane % rounds
        out[me, LANES, per + 1] = lane // rounds * (block_total * rounds // per)
        out[me, LANES, -1] = me
    return out


def per_device(tokens, norm_gain, w_qk, w_v, cotangent, log_sums, bucket_order, token_position):
    devices = lax.axis_size("tok")
    me = lax.axis_index("tok")
    size, width = tokens.shape
    rounds, heads, _ = log_sums.shape
    head_dim = width // heads
    total = bucket_order.shape[1]
    per = devices // heads
    parts = per // rounds
    chips = heads
    chip, lane = me // per, me % per
    groups = [[c * per + j for c in range(chips)] for j in range(per)]
    ring = list(range(0, chips, 2)) + list(range(chips - 1, 0, -2))

    def hop(x, distance):
        route = [
            (ring[p] * per + j, ring[(p + distance) % chips] * per + j)
            for p in range(chips)
            for j in range(per)
        ]
        return lax.ppermute(x, "tok", route)

    def swap(x, shift):
        route = [
            (c * per + j, c * per + (j + shift) % per) for c in range(chips) for j in range(per)
        ]
        return lax.ppermute(x, "tok", route)

    def send(x, distance):
        route = [
            (c * per + j, (c + distance) % chips * per + j) for c in range(chips) for j in range(per)
        ]
        return lax.ppermute(x, "tok", route)

    def exchange(x):
        return lax.all_to_all(x, "tok", 0, 0, tiled=True, axis_index_groups=groups)

    ids = lax.dynamic_index_in_dim(
        jnp.asarray(tables(devices, per, rounds, ring, total // BLOCK)), me, 0, keepdims=False
    )
    my_order = lax.dynamic_index_in_dim(bucket_order, lane % rounds, 0, keepdims=False)
    gain_row = norm_gain[None, :]
    normal, chunks = prepare(tokens, gain_row, cotangent, log_sums)

    shards = [normal]
    ahead = behind = normal
    half = chips // 2
    for s in range(1, half):
        ahead, behind = hop(ahead, 1), hop(behind, -1)
        shards += [ahead, behind]
    shards.append(
        jnp.concatenate([hop(ahead[: size // 2], 1), hop(behind[size // 2 :], -1)], axis=0)
    )
    cot = exchange(chunks)

    def my_columns(w):
        return lax.dynamic_slice_in_dim(w, chip * head_dim, head_dim, 1)

    my_weights = jnp.concatenate([my_columns(w_qk), my_columns(w_v)], axis=1)

    def project(some):
        return jnp.stack(
            [jnp.dot(n, my_weights, preferred_element_type=F32).astype(BF16) for n in some]
        )

    early = chips - 3
    qv = [project(shards[:early]), project(shards[early:])]
    qv_all = [qv] + [[swap(x, shift) for x in qv] for shift in range(1, per)]
    cot_all = [cot] + [swap(cot, shift) for shift in range(1, per)]
    sent = attention(per, parts, rounds, ids, my_order, qv_all, cot_all)
    grads = sent[0].astype(F32)
    for shift in range(1, per):
        grads = grads + swap(sent[shift], per - shift).astype(F32)
    grads = grads.astype(BF16)

    inbound = exchange(grads)
    rows = width // devices
    partials = weight_grad(per, rows, ids, grads, shards)
    mine = partials[0].astype(F32)
    for shift in range(1, per):
        mine = mine + swap(partials[shift], per - shift).astype(F32)
    mine = mine.astype(BF16)
    d_rows = [mine[0]] + [send(mine[k], k) for k in range(1, chips)]
    d_tokens, d_wqk, d_wv, gains = home(
        1.0 / math.sqrt(total), ids, inbound, d_rows, w_qk, w_v, tokens, gain_row
    )
    d_gain = gains[:, 0] / lax.dynamic_slice_in_dim(norm_gain, me * rows, rows, 0)
    return d_tokens, d_gain, d_wqk, d_wv


def solution(mesh):
    in_specs = (
        P(("groups", "tok"), None),
        P(),
        P(),
        P(),
        P(("groups", "tok"), None),
        P(None, None, ("groups", "tok")),
        P(None, "groups"),
        P(None, ("groups", "tok")),
    )
    out_specs = (
        P(("groups", "tok"), None),
        P(("groups", "tok")),
        P(("groups", "tok"), None),
        P(("groups", "tok"), None),
    )
    return jax.shard_map(
        per_device, mesh=mesh, in_specs=in_specs, out_specs=out_specs, check_vma=False
    )
```

```python
import math
from functools import partial

import jax
import jax.numpy as jnp
import numpy as np
from jax import lax
from jax.experimental import pallas as pl
from jax.experimental.pallas import tpu as pltpu
from jax.sharding import PartitionSpec as P

BLOCK = 256
EPS = 1e-06
F32 = jnp.float32
BF16 = jnp.bfloat16
TILE = 8
PITCH = 9
NN = (((1,), (0,)), ((), ()))
NT = (((1,), (1,)), ((), ()))
TN = (((0,), (0,)), ((), ()))
LANE_BYTES = 3 * 1024 * 1024
LARGE_VMEM_BYTES = 60 * 1024 * 1024
SMALL_VMEM_BYTES = 24 * 1024 * 1024
SHARDS, LANES = 0, 1


def dot(a, b, dims):
    return lax.dot_general(a, b, dims, preferred_element_type=F32)


def every(lead, size):
    return pl.ds(lead, size, stride=PITCH)


def attention_kernel(per, parts, blocks, rounds, pieces, ids, order, *refs):
    qv_refs = [refs[m * pieces : (m + 1) * pieces] for m in range(per)]
    refs = refs[per * pieces :]
    cot_refs = refs[:per]
    out_refs = refs[per : 2 * per]
    table, picked, packed, log_sums, keys, values, queries, dq, dk, dv, halo = refs[2 * per :]
    chips, size, width = out_refs[0].shape
    head_dim = width // 2
    total = table.shape[0] // PITCH
    block_total = total // BLOCK
    sum_rows = size // head_dim
    lo_start = rounds * sum_rows
    hashing = ids[LANES, per]
    first_block = ids[LANES, per + 1]

    for m in range(per):
        n = 0
        for ref in qv_refs[m]:
            for row in range(ref.shape[0]):
                base = (ids[SHARDS, n] * per + ids[LANES, m]) * (size * PITCH)
                table[every(base, size), :] = ref[row, :, :head_dim].astype(F32)
                table[every(base + 1, size), :] = ref[row, :, head_dim:].astype(F32)
                n += 1

        def fill(n, carry):
            device = n * per + ids[LANES, m]
            base = device * (size * PITCH)
            table[every(base + 2, size), :] = cot_refs[m][n, :size, :].astype(F32)
            if parts > 1:
                zero = jnp.zeros((size, head_dim), F32)
                table[every(base + 3, size), :] = zero
                table[every(base + 4, size), :] = zero
            sums = cot_refs[m][n, size:, :].astype(F32)
            sums = sums[:lo_start] + sums[lo_start : 2 * lo_start]
            chosen = sums[:sum_rows]
            for r in range(1, rounds):
                chosen = jnp.where(hashing == r, sums[r * sum_rows : (r + 1) * sum_rows], chosen)
            log_sums[device, :sum_rows, :] = chosen
            return carry

        lax.fori_loop(0, chips, fill, 0)

    def rows_of(block):
        start = lax.rem(block, block_total) * BLOCK
        for p in range(BLOCK):
            yield p * PITCH, order[start + p]

    def gather(block, slot):
        for place, row in rows_of(block):
            picked[slot, place : place + TILE, :] = table[pl.ds(row, TILE), :]

    def scatter(block, slot):
        for place, row in rows_of(block):
            table[pl.ds(row, TILE), :] = packed[slot, place : place + TILE, :]

    def load(slot):
        q = picked[slot, every(0, BLOCK), :]
        scale = lax.rsqrt(jnp.mean(q * q, axis=-1, keepdims=True) + EPS) * (1.0 / math.sqrt(head_dim))
        queries[slot] = q
        keys[slot] = (q * scale).astype(BF16)
        values[slot] = picked[slot, every(1, BLOCK), :].astype(BF16)

    def finish(slot, q, d_query, d_key, d_value):
        scale = lax.rsqrt(jnp.mean(q * q, axis=-1, keepdims=True) + EPS)
        inner = jnp.mean(q * d_key, axis=-1, keepdims=True)
        pulled = (scale * (1.0 / math.sqrt(head_dim))) * (d_key - q * (scale * scale * inner))
        packed[slot, every(3, BLOCK), :] = pulled if d_query is None else d_query + pulled
        packed[slot, every(4, BLOCK), :] = d_value

    diagonal = lax.broadcasted_iota(jnp.int32, (BLOCK, BLOCK), 0) == lax.broadcasted_iota(
        jnp.int32, (BLOCK, BLOCK), 1
    )

    def step(b, cur, first=False, write=True):
        block = first_block + b
        prev = 1 - cur
        gather(block + 1, prev)
        if write:
            scatter(block - 2, cur)
        load(cur)
        log_sum = jnp.concatenate(
            [log_sums[block, k : k + 1, :] for k in range(BLOCK // head_dim)], axis=1
        )
        cot = picked[cur, every(2, BLOCK), :].astype(BF16)
        query = queries[cur].astype(BF16)
        key_a, key_b = keys[prev], keys[cur]
        w_a = jnp.exp(dot(key_a, query, NT) - log_sum)
        p_a = w_a * dot(values[prev], cot, NT)
        w_b = jnp.where(diagonal, 0.0, jnp.exp(dot(key_b, query, NT) - log_sum))
        p_b = w_b * dot(values[cur], cot, NT)
        delta = jnp.sum(p_a + p_b, axis=0, keepdims=True)
        w_a, w_b = w_a.astype(BF16), w_b.astype(BF16)
        dv_a = dot(w_a, cot, NN)
        dv[cur] = dot(w_b, cot, NN)
        ds_a = (p_a - w_a.astype(F32) * delta).astype(BF16)
        ds_b = (p_b - w_b.astype(F32) * delta).astype(BF16)
        dk_a = dot(ds_a, query, NN)
        if first:
            halo[0] = dk_a
            halo[1] = dv_a
        else:
            finish(prev, queries[prev], dq[prev], dk[prev] + dk_a, dv[prev] + dv_a)
        dk[cur] = dot(ds_b, query, NN)
        dq[cur] = dot(ds_a, key_a, TN) + dot(ds_b, key_b, TN)

    halo_block = first_block + block_total - 1
    gather(halo_block, 1)
    load(1)
    if parts > 1:
        halo[2] = queries[1]
    gather(first_block, 0)
    step(0, 0, first=True, write=False)
    step(1, 1, write=False)

    def pair(i, carry):
        step(2 * i, 0)
        step(2 * i + 1, 1)
        return carry

    lax.fori_loop(1, blocks // 2, pair, 0)
    if blocks % 2:
        step(blocks - 1, 0)
    last = (blocks - 1) % 2
    scatter(first_block + blocks - 2, 1 - last)
    if parts == 1:
        finish(last, queries[last], dq[last], dk[last] + halo[0], dv[last] + halo[1])
    else:
        finish(1 - last, halo[2], None, halo[0], halo[1])
        scatter(halo_block, 1 - last)
        finish(last, queries[last], dq[last], dk[last], dv[last])
    scatter(first_block + blocks - 1, last)

    for m in range(per):

        def drain(n, carry):
            base = (n * per + ids[LANES, m]) * (size * PITCH)
            out_refs[m][n, :, :head_dim] = table[every(base + 3, size), :].astype(BF16)
            out_refs[m][n, :, head_dim:] = table[every(base + 4, size), :].astype(BF16)
            return carry

        lax.fori_loop(0, chips, drain, 0)


def attention(per, parts, rounds, ids, order, qv, cot):
    chips = cot[0].shape[0]
    size, width = qv[0][0].shape[1:]
    head_dim = width // 2
    total = order.shape[0]
    blocks = total // BLOCK // parts
    smem = pl.BlockSpec(memory_space=pltpu.SMEM)
    vmem = pl.BlockSpec(memory_space=pltpu.VMEM)
    flat = [piece for lane in qv for piece in lane] + list(cot)
    return pl.pallas_call(
        partial(attention_kernel, per, parts, blocks, rounds, len(qv[0])),
        out_shape=[jax.ShapeDtypeStruct((chips, size, width), BF16)] * per,
        in_specs=[smem, smem] + [vmem] * len(flat),
        out_specs=[vmem] * per,
        scratch_shapes=[
            pltpu.VMEM((total * PITCH, head_dim), F32),
            pltpu.VMEM((2, BLOCK * PITCH, head_dim), F32),
            pltpu.VMEM((2, BLOCK * PITCH, head_dim), F32),
            pltpu.VMEM((total // BLOCK, TILE, head_dim), F32),
            pltpu.VMEM((2, BLOCK, head_dim), BF16),
            pltpu.VMEM((2, BLOCK, head_dim), BF16),
            pltpu.VMEM((2, BLOCK, head_dim), F32),
            pltpu.VMEM((2, BLOCK, head_dim), F32),
            pltpu.VMEM((2, BLOCK, head_dim), F32),
            pltpu.VMEM((2, BLOCK, head_dim), F32),
            pltpu.VMEM((3, BLOCK, head_dim), F32),
        ],
        compiler_params=pltpu.CompilerParams(vmem_limit_bytes=total * PITCH * head_dim * 4 + (per + 3) * LANE_BYTES),
        name="attention",
    )(ids, order, *flat)


def prepare_kernel(tokens, gain, cot, log_sums, normal, chunks):
    heads, _, head_dim = chunks.shape
    size = tokens.shape[0]
    rounds = log_sums.shape[0]
    x = tokens[...].astype(F32)
    scale = lax.rsqrt(jnp.mean(x * x, axis=-1, keepdims=True) + EPS)
    normal[...] = (x * scale * gain[...]).astype(BF16)
    for h in range(heads):
        chunks[h, :size, :] = cot[:, h * head_dim : (h + 1) * head_dim]
        rows = [
            log_sums[r, h : h + 1, k * head_dim : (k + 1) * head_dim]
            for r in range(rounds)
            for k in range(size // head_dim)
        ]
        exact = jnp.concatenate(rows, axis=0)
        high = exact.astype(BF16).astype(F32)
        spare = jnp.zeros((chunks.shape[1] - size - 2 * len(rows), head_dim), F32)
        chunks[h, size:, :] = jnp.concatenate([high, exact - high, spare], axis=0).astype(BF16)


def prepare(tokens, gain, cot, log_sums):
    size, width = tokens.shape
    rounds, heads, _ = log_sums.shape
    head_dim = width // heads
    extra = 2 * rounds * size // head_dim
    extra = (extra + 15) // 16 * 16
    return pl.pallas_call(
        prepare_kernel,
        out_shape=[
            jax.ShapeDtypeStruct(tokens.shape, BF16),
            jax.ShapeDtypeStruct((heads, size + extra, head_dim), BF16),
        ],
        compiler_params=pltpu.CompilerParams(vmem_limit_bytes=LARGE_VMEM_BYTES),
        name="prepare",
    )(tokens, gain, cot, log_sums)


def weight_grad_kernel(per, count, ids, grads, *refs):
    shards = refs[:count]
    outs = refs[count : count + per]
    total = refs[count + per]
    chips, rows, _ = outs[0].shape
    grad_t = jnp.zeros((grads.shape[-1], shards[0].shape[-1]), F32)
    for n, shard in enumerate(shards):
        grad_t = grad_t + dot(grads[ids[SHARDS, n]], shard[...], TN)
    total[...] = grad_t.T
    for m in range(per):
        for k in range(chips):
            chip = lax.rem(ids[SHARDS, 0] + k, chips)
            start = pl.multiple_of((chip * per + ids[LANES, m]) * rows, rows)
            outs[m][k] = total[pl.ds(start, rows), :].astype(BF16)


def weight_grad(per, rows, ids, grads, shards):
    chips, _, both = grads.shape
    smem = pl.BlockSpec(memory_space=pltpu.SMEM)
    vmem = pl.BlockSpec(memory_space=pltpu.VMEM)
    return pl.pallas_call(
        partial(weight_grad_kernel, per, len(shards)),
        out_shape=[jax.ShapeDtypeStruct((chips, rows, both), BF16)] * per,
        in_specs=[smem] + [vmem] * (1 + len(shards)),
        out_specs=[vmem] * per,
        scratch_shapes=[pltpu.VMEM((shards[0].shape[1], both), F32)],
        compiler_params=pltpu.CompilerParams(vmem_limit_bytes=LARGE_VMEM_BYTES),
        name="weight_grad",
    )(ids, grads, *shards)


def home_kernel(grads, w_qk, w_v, tokens, gain, out):
    heads, _, both = grads.shape
    head_dim = both // 2
    total = jnp.zeros(tokens.shape, F32)
    for k in range(heads):
        columns = slice(k * head_dim, (k + 1) * head_dim)
        weights = jnp.concatenate([w_qk[:, columns], w_v[:, columns]], axis=1)
        total = total + dot(grads[k], weights, NT)
    x = tokens[...].astype(F32)
    scale = lax.rsqrt(jnp.mean(x * x, axis=-1, keepdims=True) + EPS)
    scaled = total * gain[...]
    inner = jnp.mean(x * scaled, axis=-1, keepdims=True)
    out[...] = (scale * (scaled - x * (scale * scale * inner))).astype(BF16)


def home(grads, w_qk, w_v, tokens, gain):
    return pl.pallas_call(
        home_kernel,
        out_shape=jax.ShapeDtypeStruct(tokens.shape, BF16),
        compiler_params=pltpu.CompilerParams(vmem_limit_bytes=SMALL_VMEM_BYTES),
        name="home",
    )(grads, w_qk, w_v, tokens, gain)


def rows_kernel(scale_out, ids, qk_own, v_own, own_gain, *refs):
    d_rows = refs[:-3]
    d_wqk, d_wv, d_gain = refs[-3:]
    heads = len(d_rows)
    rows, both = d_rows[0].shape
    head_dim = both // 2
    gains = jnp.zeros((rows, head_dim), F32)
    for k in range(heads):
        source = lax.rem(ids[SHARDS, 0] + heads - k, heads)
        columns = pl.ds(pl.multiple_of(source * head_dim, head_dim), head_dim)
        qk_rows = d_rows[k][:, :head_dim].astype(F32) * scale_out
        v_rows = d_rows[k][:, head_dim:].astype(F32) * scale_out
        d_wqk[:, columns] = qk_rows
        d_wv[:, columns] = v_rows
        gains = gains + qk_rows * qk_own[:, columns].astype(F32)
        gains = gains + v_rows * v_own[:, columns].astype(F32)
    d_gain[...] = jnp.sum(gains.T, axis=0, keepdims=True) / own_gain[...]


def weight_rows(scale_out, ids, d_rows, qk_own, v_own, own_gain):
    rows, width = qk_own.shape
    smem = pl.BlockSpec(memory_space=pltpu.SMEM)
    vmem = pl.BlockSpec(memory_space=pltpu.VMEM)
    return pl.pallas_call(
        partial(rows_kernel, scale_out),
        out_shape=[
            jax.ShapeDtypeStruct((rows, width), F32),
            jax.ShapeDtypeStruct((rows, width), F32),
            jax.ShapeDtypeStruct((1, rows), F32),
        ],
        in_specs=[smem] + [vmem] * (3 + len(d_rows)),
        out_specs=[vmem] * 3,
        compiler_params=pltpu.CompilerParams(vmem_limit_bytes=SMALL_VMEM_BYTES),
        name="weight_rows",
    )(ids, qk_own, v_own, own_gain, *d_rows)


def tables(devices, per, rounds, ring, block_total):
    chips = len(ring)
    place = [ring.index(c) for c in range(chips)]
    steps = [0]
    for s in range(1, chips // 2):
        steps += [-s, s]
    steps.append(chips // 2)
    out = np.zeros((devices, 2, max(chips, per + 3)), np.int32)
    for me in range(devices):
        chip, lane = me // per, me % per
        out[me, SHARDS, :chips] = [ring[(place[chip] + s) % chips] for s in steps]
        out[me, LANES, :per] = [(lane - m) % per for m in range(per)]
        out[me, LANES, per] = lane % rounds
        out[me, LANES, per + 1] = lane // rounds * (block_total * rounds // per)
        out[me, LANES, -1] = me
    return out


def per_device(tokens, norm_gain, w_qk, w_v, cotangent, log_sums, bucket_order, token_position):
    devices = lax.axis_size("tok")
    me = lax.axis_index("tok")
    size, width = tokens.shape
    rounds, heads, _ = log_sums.shape
    head_dim = width // heads
    total = bucket_order.shape[1]
    per = devices // heads
    parts = per // rounds
    chips = heads
    chip, lane = me // per, me % per
    groups = [[c * per + j for c in range(chips)] for j in range(per)]
    ring = list(range(0, chips, 2)) + list(range(chips - 1, 0, -2))

    def hop(x, distance):
        route = [
            (ring[p] * per + j, ring[(p + distance) % chips] * per + j)
            for p in range(chips)
            for j in range(per)
        ]
        return lax.ppermute(x, "tok", route)

    def swap(x, shift):
        route = [
            (c * per + j, c * per + (j + shift) % per) for c in range(chips) for j in range(per)
        ]
        return lax.ppermute(x, "tok", route)

    def send(x, distance):
        route = [
            (c * per + j, (c + distance) % chips * per + j) for c in range(chips) for j in range(per)
        ]
        return lax.ppermute(x, "tok", route)

    def exchange(x):
        return lax.all_to_all(x, "tok", 0, 0, tiled=True, axis_index_groups=groups)

    ids = lax.dynamic_index_in_dim(
        jnp.asarray(tables(devices, per, rounds, ring, total // BLOCK)), me, 0, keepdims=False
    )
    my_order = PITCH * lax.dynamic_index_in_dim(bucket_order, lane % rounds, 0, keepdims=False)
    gain_row = norm_gain[None, :]
    normal, chunks = prepare(tokens, gain_row, cotangent, log_sums)

    shards = [normal]
    ahead = behind = normal
    half = chips // 2
    for s in range(1, half):
        ahead, behind = hop(ahead, 1), hop(behind, -1)
        shards += [ahead, behind]
    shards.append(
        jnp.concatenate([hop(ahead[: size // 2], 1), hop(behind[size // 2 :], -1)], axis=0)
    )
    cot = exchange(chunks)

    def my_columns(w):
        return lax.dynamic_slice_in_dim(w, chip * head_dim, head_dim, 1)

    my_weights = jnp.concatenate([my_columns(w_qk), my_columns(w_v)], axis=1)

    rows = width // devices
    qk_own, v_own, own_gain = [
        lax.dynamic_slice_in_dim(v, me * rows, rows, 0) for v in (w_qk, w_v, norm_gain)
    ]
    shards[0], ids, my_order, qk_own, v_own, own_gain = lax.optimization_barrier(
        (shards[0], ids, my_order, qk_own, v_own, own_gain)
    )

    def project(some):
        return jnp.stack(
            [jnp.dot(n, my_weights, preferred_element_type=F32).astype(BF16) for n in some]
        )

    early = chips - 3
    qv = [project(shards[:early]), project(shards[early:-1]), project(shards[-1:])]
    qv_all = [qv] + [[swap(x, shift) for x in qv] for shift in range(1, per)]
    cot_all = [cot] + [swap(cot, shift) for shift in range(1, per)]
    sent = attention(per, parts, rounds, ids, my_order, qv_all, cot_all)
    grads = sent[0].astype(F32)
    for shift in range(1, per):
        grads = grads + swap(sent[shift], per - shift).astype(F32)
    grads = grads.astype(BF16)
    inbound = exchange(grads)
    partials = weight_grad(per, rows, ids, grads, shards)
    mine = partials[0].astype(F32)
    for shift in range(1, per):
        mine = mine + swap(partials[shift], per - shift).astype(F32)
    mine = mine.astype(BF16)
    d_rows = [mine[0]] + [send(mine[k], k) for k in range(1, chips)]
    d_tokens = home(inbound, w_qk, w_v, tokens, gain_row)
    d_wqk, d_wv, d_gain = weight_rows(
        1.0 / math.sqrt(total), ids, d_rows, qk_own, v_own, own_gain[None, :]
    )
    return d_tokens, d_gain.reshape(rows), d_wqk, d_wv


def solution(mesh):
    in_specs = (
        P(("groups", "tok"), None),
        P(),
        P(),
        P(),
        P(("groups", "tok"), None),
        P(None, None, ("groups", "tok")),
        P(None, "groups"),
        P(None, ("groups", "tok")),
    )
    out_specs = (
        P(("groups", "tok"), None),
        P(("groups", "tok")),
        P(("groups", "tok"), None),
        P(("groups", "tok"), None),
    )
    return jax.shard_map(
        per_device, mesh=mesh, in_specs=in_specs, out_specs=out_specs, check_vma=False
    )
```

```python
import math
from functools import partial

import jax
import jax.numpy as jnp
import numpy as np
from jax import lax
from jax.experimental import pallas as pl
from jax.experimental.pallas import tpu as pltpu
from jax.sharding import PartitionSpec as P

BLOCK = 256
EPS = 1e-06
F32 = jnp.float32
BF16 = jnp.bfloat16
TILE = 8
PITCH = 9
NN = (((1,), (0,)), ((), ()))
NT = (((1,), (1,)), ((), ()))
TN = (((0,), (0,)), ((), ()))
LANE_BYTES = 3 * 1024 * 1024
LARGE_VMEM_BYTES = 60 * 1024 * 1024
SMALL_VMEM_BYTES = 24 * 1024 * 1024
SHARDS, LANES = 0, 1


def dot(a, b, dims):
    return lax.dot_general(a, b, dims, preferred_element_type=F32)


def every(lead, size):
    return pl.ds(lead, size, stride=PITCH)


def attention_kernel(per, parts, blocks, rounds, pieces, ids, order, *refs):
    qv_refs = [refs[m * pieces : (m + 1) * pieces] for m in range(per)]
    refs = refs[per * pieces :]
    cot_refs = refs[:per]
    out_refs = refs[per : 2 * per]
    table, picked, packed, log_sums, keys, values, queries, dq, dk, dv, halo = refs[2 * per :]
    chips, size, width = out_refs[0].shape
    head_dim = width // 2
    total = table.shape[0] // PITCH
    block_total = total // BLOCK
    sum_rows = size // head_dim
    lo_start = rounds * sum_rows
    hashing = ids[LANES, per]
    first_block = ids[LANES, per + 1]

    for m in range(per):
        n = 0
        for ref in qv_refs[m]:
            for row in range(ref.shape[0]):
                base = (ids[SHARDS, n] * per + ids[LANES, m]) * (size * PITCH)
                table[every(base, size), :] = ref[row, :, :head_dim].astype(F32)
                table[every(base + 1, size), :] = ref[row, :, head_dim:].astype(F32)
                n += 1

        def fill(n, carry):
            device = n * per + ids[LANES, m]
            base = device * (size * PITCH)
            table[every(base + 2, size), :] = cot_refs[m][n, :size, :].astype(F32)
            if parts > 1:
                zero = jnp.zeros((size, head_dim), F32)
                table[every(base + 3, size), :] = zero
                table[every(base + 4, size), :] = zero
            sums = cot_refs[m][n, size:, :].astype(F32)
            sums = sums[:lo_start] + sums[lo_start : 2 * lo_start]
            chosen = sums[:sum_rows]
            for r in range(1, rounds):
                chosen = jnp.where(hashing == r, sums[r * sum_rows : (r + 1) * sum_rows], chosen)
            log_sums[device, :sum_rows, :] = chosen
            return carry

        lax.fori_loop(0, chips, fill, 0)

    def rows_of(block):
        start = lax.rem(block, block_total) * BLOCK
        for p in range(BLOCK):
            yield p * PITCH, order[start + p]

    def gather(block, slot):
        for place, row in rows_of(block):
            picked[slot, place : place + TILE, :] = table[pl.ds(row, TILE), :]

    def scatter(block, slot):
        for place, row in rows_of(block):
            table[pl.ds(row, TILE), :] = packed[slot, place : place + TILE, :]

    def load(slot):
        q = picked[slot, every(0, BLOCK), :]
        scale = lax.rsqrt(jnp.mean(q * q, axis=-1, keepdims=True) + EPS) * (1.0 / math.sqrt(head_dim))
        queries[slot] = q
        keys[slot] = (q * scale).astype(BF16)
        values[slot] = picked[slot, every(1, BLOCK), :].astype(BF16)

    def finish(slot, q, d_query, d_key, d_value):
        scale = lax.rsqrt(jnp.mean(q * q, axis=-1, keepdims=True) + EPS)
        inner = jnp.mean(q * d_key, axis=-1, keepdims=True)
        pulled = (scale * (1.0 / math.sqrt(head_dim))) * (d_key - q * (scale * scale * inner))
        packed[slot, every(3, BLOCK), :] = pulled if d_query is None else d_query + pulled
        packed[slot, every(4, BLOCK), :] = d_value

    diagonal = lax.broadcasted_iota(jnp.int32, (BLOCK, BLOCK), 0) == lax.broadcasted_iota(
        jnp.int32, (BLOCK, BLOCK), 1
    )

    def step(b, cur, first=False, write=True):
        block = first_block + b
        prev = 1 - cur
        gather(block + 1, prev)
        if write:
            scatter(block - 2, cur)
        load(cur)
        log_sum = jnp.concatenate(
            [log_sums[block, k : k + 1, :] for k in range(BLOCK // head_dim)], axis=1
        )
        cot = picked[cur, every(2, BLOCK), :].astype(BF16)
        query = queries[cur].astype(BF16)
        key_a, key_b = keys[prev], keys[cur]
        w_a = jnp.exp(dot(key_a, query, NT) - log_sum)
        p_a = w_a * dot(values[prev], cot, NT)
        w_b = jnp.where(diagonal, 0.0, jnp.exp(dot(key_b, query, NT) - log_sum))
        p_b = w_b * dot(values[cur], cot, NT)
        delta = jnp.sum(p_a + p_b, axis=0, keepdims=True)
        w_a, w_b = w_a.astype(BF16), w_b.astype(BF16)
        dv_a = dot(w_a, cot, NN)
        dv[cur] = dot(w_b, cot, NN)
        ds_a = (p_a - w_a.astype(F32) * delta).astype(BF16)
        ds_b = (p_b - w_b.astype(F32) * delta).astype(BF16)
        dk_a = dot(ds_a, query, NN)
        if first:
            halo[0] = dk_a
            halo[1] = dv_a
        else:
            finish(prev, queries[prev], dq[prev], dk[prev] + dk_a, dv[prev] + dv_a)
        dk[cur] = dot(ds_b, query, NN)
        dq[cur] = dot(ds_a, key_a, TN) + dot(ds_b, key_b, TN)

    halo_block = first_block + block_total - 1
    gather(halo_block, 1)
    load(1)
    if parts > 1:
        halo[2] = queries[1]
    gather(first_block, 0)
    step(0, 0, first=True, write=False)
    step(1, 1, write=False)

    def pair(i, carry):
        step(2 * i, 0)
        step(2 * i + 1, 1)
        return carry

    lax.fori_loop(1, blocks // 2, pair, 0)
    if blocks % 2:
        step(blocks - 1, 0)
    last = (blocks - 1) % 2
    scatter(first_block + blocks - 2, 1 - last)
    if parts == 1:
        finish(last, queries[last], dq[last], dk[last] + halo[0], dv[last] + halo[1])
    else:
        finish(1 - last, halo[2], None, halo[0], halo[1])
        scatter(halo_block, 1 - last)
        finish(last, queries[last], dq[last], dk[last], dv[last])
    scatter(first_block + blocks - 1, last)

    for m in range(per):

        def drain(n, carry):
            base = (n * per + ids[LANES, m]) * (size * PITCH)
            out_refs[m][n, :, :head_dim] = table[every(base + 3, size), :].astype(BF16)
            out_refs[m][n, :, head_dim:] = table[every(base + 4, size), :].astype(BF16)
            return carry

        lax.fori_loop(0, chips, drain, 0)


def attention(per, parts, rounds, ids, order, qv, cot):
    chips = cot[0].shape[0]
    size, width = qv[0][0].shape[1:]
    head_dim = width // 2
    total = order.shape[0]
    blocks = total // BLOCK // parts
    smem = pl.BlockSpec(memory_space=pltpu.SMEM)
    vmem = pl.BlockSpec(memory_space=pltpu.VMEM)
    flat = [piece for lane in qv for piece in lane] + list(cot)
    return pl.pallas_call(
        partial(attention_kernel, per, parts, blocks, rounds, len(qv[0])),
        out_shape=[jax.ShapeDtypeStruct((chips, size, width), BF16)] * per,
        in_specs=[smem, smem] + [vmem] * len(flat),
        out_specs=[vmem] * per,
        scratch_shapes=[
            pltpu.VMEM((total * PITCH, head_dim), F32),
            pltpu.VMEM((2, BLOCK * PITCH, head_dim), F32),
            pltpu.VMEM((2, BLOCK * PITCH, head_dim), F32),
            pltpu.VMEM((total // BLOCK, TILE, head_dim), F32),
            pltpu.VMEM((2, BLOCK, head_dim), BF16),
            pltpu.VMEM((2, BLOCK, head_dim), BF16),
            pltpu.VMEM((2, BLOCK, head_dim), F32),
            pltpu.VMEM((2, BLOCK, head_dim), F32),
            pltpu.VMEM((2, BLOCK, head_dim), F32),
            pltpu.VMEM((2, BLOCK, head_dim), F32),
            pltpu.VMEM((3, BLOCK, head_dim), F32),
        ],
        compiler_params=pltpu.CompilerParams(vmem_limit_bytes=total * PITCH * head_dim * 4 + (per + 3) * LANE_BYTES),
        name="attention",
    )(ids, order, *flat)


def prepare_kernel(tokens, gain, cot, log_sums, normal, chunks):
    heads, _, head_dim = chunks.shape
    size = tokens.shape[0]
    rounds = log_sums.shape[0]
    x = tokens[...].astype(F32)
    scale = lax.rsqrt(jnp.mean(x * x, axis=-1, keepdims=True) + EPS)
    normal[...] = (x * scale * gain[...]).astype(BF16)
    for h in range(heads):
        chunks[h, :size, :] = cot[:, h * head_dim : (h + 1) * head_dim]
        rows = [
            log_sums[r, h : h + 1, k * head_dim : (k + 1) * head_dim]
            for r in range(rounds)
            for k in range(size // head_dim)
        ]
        exact = jnp.concatenate(rows, axis=0)
        high = exact.astype(BF16).astype(F32)
        spare = jnp.zeros((chunks.shape[1] - size - 2 * len(rows), head_dim), F32)
        chunks[h, size:, :] = jnp.concatenate([high, exact - high, spare], axis=0).astype(BF16)


def prepare(tokens, gain, cot, log_sums):
    size, width = tokens.shape
    rounds, heads, _ = log_sums.shape
    head_dim = width // heads
    extra = 2 * rounds * size // head_dim
    extra = (extra + 15) // 16 * 16
    return pl.pallas_call(
        prepare_kernel,
        out_shape=[
            jax.ShapeDtypeStruct(tokens.shape, BF16),
            jax.ShapeDtypeStruct((heads, size + extra, head_dim), BF16),
        ],
        compiler_params=pltpu.CompilerParams(vmem_limit_bytes=LARGE_VMEM_BYTES),
        name="prepare",
    )(tokens, gain, cot, log_sums)


def weight_grad_kernel(per, count, ids, grads, *refs):
    shards = refs[:count]
    outs = refs[count : count + per]
    total = refs[count + per]
    chips, rows, _ = outs[0].shape
    grad_t = jnp.zeros((grads.shape[-1], shards[0].shape[-1]), F32)
    for n, shard in enumerate(shards):
        grad_t = grad_t + dot(grads[ids[SHARDS, n]], shard[...], TN)
    total[...] = grad_t.T
    for m in range(per):
        for k in range(chips):
            chip = lax.rem(ids[SHARDS, 0] + k, chips)
            start = pl.multiple_of((chip * per + ids[LANES, m]) * rows, rows)
            outs[m][k] = total[pl.ds(start, rows), :].astype(BF16)


def weight_grad(per, rows, ids, grads, shards):
    chips, _, both = grads.shape
    smem = pl.BlockSpec(memory_space=pltpu.SMEM)
    vmem = pl.BlockSpec(memory_space=pltpu.VMEM)
    return pl.pallas_call(
        partial(weight_grad_kernel, per, len(shards)),
        out_shape=[jax.ShapeDtypeStruct((chips, rows, both), BF16)] * per,
        in_specs=[smem] + [vmem] * (1 + len(shards)),
        out_specs=[vmem] * per,
        scratch_shapes=[pltpu.VMEM((shards[0].shape[1], both), F32)],
        compiler_params=pltpu.CompilerParams(vmem_limit_bytes=LARGE_VMEM_BYTES),
        name="weight_grad",
    )(ids, grads, *shards)


def home_kernel(grads, w_qk, w_v, tokens, gain, out):
    heads, _, both = grads.shape
    head_dim = both // 2
    total = jnp.zeros(tokens.shape, F32)
    for k in range(heads):
        columns = slice(k * head_dim, (k + 1) * head_dim)
        weights = jnp.concatenate([w_qk[:, columns], w_v[:, columns]], axis=1)
        total = total + dot(grads[k], weights, NT)
    x = tokens[...].astype(F32)
    scale = lax.rsqrt(jnp.mean(x * x, axis=-1, keepdims=True) + EPS)
    scaled = total * gain[...]
    inner = jnp.mean(x * scaled, axis=-1, keepdims=True)
    out[...] = (scale * (scaled - x * (scale * scale * inner))).astype(BF16)


def home(grads, w_qk, w_v, tokens, gain):
    return pl.pallas_call(
        home_kernel,
        out_shape=jax.ShapeDtypeStruct(tokens.shape, BF16),
        compiler_params=pltpu.CompilerParams(vmem_limit_bytes=SMALL_VMEM_BYTES),
        name="home",
    )(grads, w_qk, w_v, tokens, gain)


def rows_kernel(scale_out, ids, qk_own, v_own, own_gain, *refs):
    d_rows = refs[:-3]
    d_wqk, d_wv, d_gain = refs[-3:]
    heads = len(d_rows)
    rows, both = d_rows[0].shape
    head_dim = both // 2
    gains = jnp.zeros((rows, head_dim), F32)
    for k in range(heads):
        source = lax.rem(ids[SHARDS, 0] + heads - k, heads)
        columns = pl.ds(pl.multiple_of(source * head_dim, head_dim), head_dim)
        qk_rows = d_rows[k][:, :head_dim].astype(F32) * scale_out
        v_rows = d_rows[k][:, head_dim:].astype(F32) * scale_out
        d_wqk[:, columns] = qk_rows
        d_wv[:, columns] = v_rows
        gains = gains + qk_rows * qk_own[:, columns].astype(F32)
        gains = gains + v_rows * v_own[:, columns].astype(F32)
    d_gain[...] = jnp.sum(gains.T, axis=0, keepdims=True) / own_gain[...]


def weight_rows(scale_out, ids, d_rows, qk_own, v_own, own_gain):
    rows, width = qk_own.shape
    smem = pl.BlockSpec(memory_space=pltpu.SMEM)
    vmem = pl.BlockSpec(memory_space=pltpu.VMEM)
    return pl.pallas_call(
        partial(rows_kernel, scale_out),
        out_shape=[
            jax.ShapeDtypeStruct((rows, width), F32),
            jax.ShapeDtypeStruct((rows, width), F32),
            jax.ShapeDtypeStruct((1, rows), F32),
        ],
        in_specs=[smem] + [vmem] * (3 + len(d_rows)),
        out_specs=[vmem] * 3,
        compiler_params=pltpu.CompilerParams(vmem_limit_bytes=SMALL_VMEM_BYTES),
        name="weight_rows",
    )(ids, qk_own, v_own, own_gain, *d_rows)


def tables(devices, per, rounds, ring, block_total):
    chips = len(ring)
    place = [ring.index(c) for c in range(chips)]
    steps = [0]
    for s in range(1, chips // 2):
        steps += [-s, s]
    steps.append(chips // 2)
    out = np.zeros((devices, 2, max(chips, per + 3)), np.int32)
    for me in range(devices):
        chip, lane = me // per, me % per
        out[me, SHARDS, :chips] = [ring[(place[chip] + s) % chips] for s in steps]
        out[me, LANES, :per] = [(lane - m) % per for m in range(per)]
        out[me, LANES, per] = lane % rounds
        out[me, LANES, per + 1] = lane // rounds * (block_total * rounds // per)
        out[me, LANES, -1] = me
    return out


def per_device(tokens, norm_gain, w_qk, w_v, cotangent, log_sums, bucket_order, token_position):
    devices = lax.axis_size("tok")
    me = lax.axis_index("tok")
    size, width = tokens.shape
    rounds, heads, _ = log_sums.shape
    head_dim = width // heads
    total = bucket_order.shape[1]
    per = devices // heads
    parts = per // rounds
    chips = heads
    chip, lane = me // per, me % per
    groups = [[c * per + j for c in range(chips)] for j in range(per)]
    ring = list(range(0, chips, 2)) + list(range(chips - 1, 0, -2))

    def hop(x, distance):
        route = [
            (ring[p] * per + j, ring[(p + distance) % chips] * per + j)
            for p in range(chips)
            for j in range(per)
        ]
        return lax.ppermute(x, "tok", route)

    def swap(x, shift):
        route = [
            (c * per + j, c * per + (j + shift) % per) for c in range(chips) for j in range(per)
        ]
        return lax.ppermute(x, "tok", route)

    def send(x, distance):
        route = [
            (c * per + j, (c + distance) % chips * per + j) for c in range(chips) for j in range(per)
        ]
        return lax.ppermute(x, "tok", route)

    def exchange(x):
        return lax.all_to_all(x, "tok", 0, 0, tiled=True, axis_index_groups=groups)

    ids = lax.dynamic_index_in_dim(
        jnp.asarray(tables(devices, per, rounds, ring, total // BLOCK)), me, 0, keepdims=False
    )
    my_order = PITCH * lax.dynamic_index_in_dim(bucket_order, lane % rounds, 0, keepdims=False)
    gain_row = norm_gain[None, :]
    normal, chunks = prepare(tokens, gain_row, cotangent, log_sums)

    shards = [normal]
    ahead = behind = normal
    half = chips // 2
    for s in range(1, half):
        ahead, behind = hop(ahead, 1), hop(behind, -1)
        shards += [ahead, behind]
    shards.append(
        jnp.concatenate([hop(ahead[: size // 2], 1), hop(behind[size // 2 :], -1)], axis=0)
    )
    cot = exchange(chunks)

    def my_columns(w):
        return lax.dynamic_slice_in_dim(w, chip * head_dim, head_dim, 1)

    my_weights = jnp.concatenate([my_columns(w_qk), my_columns(w_v)], axis=1)

    rows = width // devices
    qk_own, v_own, own_gain = [
        lax.dynamic_slice_in_dim(v, me * rows, rows, 0) for v in (w_qk, w_v, norm_gain)
    ]
    shards[0], ids, my_order, qk_own, v_own, own_gain = lax.optimization_barrier(
        (shards[0], ids, my_order, qk_own, v_own, own_gain)
    )

    def project(some):
        return jnp.stack(
            [jnp.dot(n, my_weights, preferred_element_type=F32).astype(BF16) for n in some]
        )

    early = chips - 3
    qv = [project(shards[:early]), project(shards[early:-1]), project(shards[-1:])]
    qv_all = [qv] + [[swap(x, shift) for x in qv] for shift in range(1, per)]
    cot_all = [cot] + [swap(cot, shift) for shift in range(1, per)]
    sent = attention(per, parts, rounds, ids, my_order, qv_all, cot_all)
    grads = sent[0].astype(F32)
    for shift in range(1, per):
        grads = grads + swap(sent[shift], per - shift).astype(F32)
    grads = grads.astype(BF16)
    inbound = exchange(grads)
    partials = weight_grad(per, rows, ids, grads, shards)
    mine = partials[0].astype(F32)
    for shift in range(1, per):
        mine = mine + swap(partials[shift], per - shift).astype(F32)
    mine = mine.astype(BF16)
    d_rows = [mine[0]] + [send(mine[k], k) for k in range(1, chips)]
    d_tokens = home(inbound, w_qk, w_v, tokens, gain_row)
    *d_rows, d_tokens = lax.optimization_barrier((*d_rows, d_tokens))
    d_wqk, d_wv, d_gain = weight_rows(
        1.0 / math.sqrt(total), ids, d_rows, qk_own, v_own, own_gain[None, :]
    )
    return d_tokens, d_gain.reshape(rows), d_wqk, d_wv


def solution(mesh):
    in_specs = (
        P(("groups", "tok"), None),
        P(),
        P(),
        P(),
        P(("groups", "tok"), None),
        P(None, None, ("groups", "tok")),
        P(None, "groups"),
        P(None, ("groups", "tok")),
    )
    out_specs = (
        P(("groups", "tok"), None),
        P(("groups", "tok")),
        P(("groups", "tok"), None),
        P(("groups", "tok"), None),
    )
    return jax.shard_map(
        per_device, mesh=mesh, in_specs=in_specs, out_specs=out_specs, check_vma=False
    )
```

```python
import math
from functools import partial

import jax
import jax.numpy as jnp
import numpy as np
from jax import lax
from jax.experimental import pallas as pl
from jax.experimental.pallas import tpu as pltpu
from jax.sharding import PartitionSpec as P

BLOCK = 256
EPS = 1e-06
F32 = jnp.float32
BF16 = jnp.bfloat16
TILE = 8
PITCH = 9
NN = (((1,), (0,)), ((), ()))
NT = (((1,), (1,)), ((), ()))
TN = (((0,), (0,)), ((), ()))
LANE_BYTES = 3 * 1024 * 1024
LARGE_VMEM_BYTES = 60 * 1024 * 1024
SMALL_VMEM_BYTES = 24 * 1024 * 1024
SHARDS, LANES = 0, 1


def dot(a, b, dims):
    return lax.dot_general(a, b, dims, preferred_element_type=F32)


def every(lead, size):
    return pl.ds(lead, size, stride=PITCH)


def attention_kernel(per, parts, blocks, rounds, pieces, ids, order, *refs):
    qv_refs = [refs[m * pieces : (m + 1) * pieces] for m in range(per)]
    refs = refs[per * pieces :]
    cot_refs = refs[:per]
    out_refs = refs[per : 2 * per]
    table, picked, packed, log_sums, keys, values, queries, dq, dk, dv, halo = refs[2 * per :]
    chips, size, width = out_refs[0].shape
    head_dim = width // 2
    total = table.shape[0] // PITCH
    block_total = total // BLOCK
    sum_rows = size // head_dim
    lo_start = rounds * sum_rows
    hashing = ids[LANES, per]
    first_block = ids[LANES, per + 1]

    for m in range(per):
        n = 0
        for ref in qv_refs[m]:
            for row in range(ref.shape[0]):
                base = (ids[SHARDS, n] * per + ids[LANES, m]) * (size * PITCH)
                table[every(base, size), :] = ref[row, :, :head_dim].astype(F32)
                table[every(base + 1, size), :] = ref[row, :, head_dim:].astype(F32)
                n += 1

        def fill(n, carry):
            device = n * per + ids[LANES, m]
            base = device * (size * PITCH)
            table[every(base + 2, size), :] = cot_refs[m][n, :size, :].astype(F32)
            if parts > 1:
                zero = jnp.zeros((size, head_dim), F32)
                table[every(base + 3, size), :] = zero
                table[every(base + 4, size), :] = zero
            sums = cot_refs[m][n, size:, :].astype(F32)
            sums = sums[:lo_start] + sums[lo_start : 2 * lo_start]
            chosen = sums[:sum_rows]
            for r in range(1, rounds):
                chosen = jnp.where(hashing == r, sums[r * sum_rows : (r + 1) * sum_rows], chosen)
            log_sums[device, :sum_rows, :] = chosen
            return carry

        lax.fori_loop(0, chips, fill, 0)

    def rows_of(block):
        start = lax.rem(block, block_total) * BLOCK
        for p in range(BLOCK):
            yield p * PITCH, order[start + p]

    def gather(block, slot):
        for place, row in rows_of(block):
            picked[slot, place : place + TILE, :] = table[pl.ds(row, TILE), :]

    def scatter(block, slot):
        for place, row in rows_of(block):
            table[pl.ds(row, TILE), :] = packed[slot, place : place + TILE, :]

    def load(slot):
        q = picked[slot, every(0, BLOCK), :]
        scale = lax.rsqrt(jnp.mean(q * q, axis=-1, keepdims=True) + EPS) * (1.0 / math.sqrt(head_dim))
        queries[slot] = q
        keys[slot] = (q * scale).astype(BF16)
        values[slot] = picked[slot, every(1, BLOCK), :].astype(BF16)

    def finish(slot, q, d_query, d_key, d_value):
        scale = lax.rsqrt(jnp.mean(q * q, axis=-1, keepdims=True) + EPS)
        inner = jnp.mean(q * d_key, axis=-1, keepdims=True)
        pulled = (scale * (1.0 / math.sqrt(head_dim))) * (d_key - q * (scale * scale * inner))
        packed[slot, every(3, BLOCK), :] = pulled if d_query is None else d_query + pulled
        packed[slot, every(4, BLOCK), :] = d_value

    diagonal = lax.broadcasted_iota(jnp.int32, (BLOCK, BLOCK), 0) == lax.broadcasted_iota(
        jnp.int32, (BLOCK, BLOCK), 1
    )

    def step(b, cur, first=False, write=True):
        block = first_block + b
        prev = 1 - cur
        gather(block + 1, prev)
        if write:
            scatter(block - 2, cur)
        load(cur)
        log_sum = jnp.concatenate(
            [log_sums[block, k : k + 1, :] for k in range(BLOCK // head_dim)], axis=1
        )
        cot = picked[cur, every(2, BLOCK), :].astype(BF16)
        query = queries[cur].astype(BF16)
        key_a, key_b = keys[prev], keys[cur]
        w_a = jnp.exp(dot(key_a, query, NT) - log_sum)
        p_a = w_a * dot(values[prev], cot, NT)
        w_b = jnp.where(diagonal, 0.0, jnp.exp(dot(key_b, query, NT) - log_sum))
        p_b = w_b * dot(values[cur], cot, NT)
        delta = jnp.sum(p_a + p_b, axis=0, keepdims=True)
        w_a, w_b = w_a.astype(BF16), w_b.astype(BF16)
        dv_a = dot(w_a, cot, NN)
        dv[cur] = dot(w_b, cot, NN)
        ds_a = (p_a - w_a.astype(F32) * delta).astype(BF16)
        ds_b = (p_b - w_b.astype(F32) * delta).astype(BF16)
        dk_a = dot(ds_a, query, NN)
        if first:
            halo[0] = dk_a
            halo[1] = dv_a
        else:
            finish(prev, queries[prev], dq[prev], dk[prev] + dk_a, dv[prev] + dv_a)
        dk[cur] = dot(ds_b, query, NN)
        dq[cur] = dot(ds_a, key_a, TN) + dot(ds_b, key_b, TN)

    halo_block = first_block + block_total - 1
    gather(halo_block, 1)
    load(1)
    if parts > 1:
        halo[2] = queries[1]
    gather(first_block, 0)
    step(0, 0, first=True, write=False)
    step(1, 1, write=False)

    def pair(i, carry):
        step(2 * i, 0)
        step(2 * i + 1, 1)
        return carry

    lax.fori_loop(1, blocks // 2, pair, 0)
    if blocks % 2:
        step(blocks - 1, 0)
    last = (blocks - 1) % 2
    scatter(first_block + blocks - 2, 1 - last)
    if parts == 1:
        finish(last, queries[last], dq[last], dk[last] + halo[0], dv[last] + halo[1])
    else:
        finish(1 - last, halo[2], None, halo[0], halo[1])
        scatter(halo_block, 1 - last)
        finish(last, queries[last], dq[last], dk[last], dv[last])
    scatter(first_block + blocks - 1, last)

    for m in range(per):

        def drain(n, carry):
            base = (n * per + ids[LANES, m]) * (size * PITCH)
            out_refs[m][n, :, :head_dim] = table[every(base + 3, size), :].astype(BF16)
            out_refs[m][n, :, head_dim:] = table[every(base + 4, size), :].astype(BF16)
            return carry

        lax.fori_loop(0, chips, drain, 0)


def attention(per, parts, rounds, ids, order, qv, cot):
    chips = cot[0].shape[0]
    size, width = qv[0][0].shape[1:]
    head_dim = width // 2
    total = order.shape[0]
    blocks = total // BLOCK // parts
    smem = pl.BlockSpec(memory_space=pltpu.SMEM)
    vmem = pl.BlockSpec(memory_space=pltpu.VMEM)
    flat = [piece for lane in qv for piece in lane] + list(cot)
    return pl.pallas_call(
        partial(attention_kernel, per, parts, blocks, rounds, len(qv[0])),
        out_shape=[jax.ShapeDtypeStruct((chips, size, width), BF16)] * per,
        in_specs=[smem, smem] + [vmem] * len(flat),
        out_specs=[vmem] * per,
        scratch_shapes=[
            pltpu.VMEM((total * PITCH, head_dim), F32),
            pltpu.VMEM((2, BLOCK * PITCH, head_dim), F32),
            pltpu.VMEM((2, BLOCK * PITCH, head_dim), F32),
            pltpu.VMEM((total // BLOCK, TILE, head_dim), F32),
            pltpu.VMEM((2, BLOCK, head_dim), BF16),
            pltpu.VMEM((2, BLOCK, head_dim), BF16),
            pltpu.VMEM((2, BLOCK, head_dim), F32),
            pltpu.VMEM((2, BLOCK, head_dim), F32),
            pltpu.VMEM((2, BLOCK, head_dim), F32),
            pltpu.VMEM((2, BLOCK, head_dim), F32),
            pltpu.VMEM((3, BLOCK, head_dim), F32),
        ],
        compiler_params=pltpu.CompilerParams(vmem_limit_bytes=total * PITCH * head_dim * 4 + (per + 3) * LANE_BYTES),
        name="attention",
    )(ids, order, *flat)


def prepare_kernel(tokens, gain, cot, log_sums, normal, chunks):
    heads, _, head_dim = chunks.shape
    size = tokens.shape[0]
    rounds = log_sums.shape[0]
    x = tokens[...].astype(F32)
    scale = lax.rsqrt(jnp.mean(x * x, axis=-1, keepdims=True) + EPS)
    normal[...] = (x * scale * gain[...]).astype(BF16)
    for h in range(heads):
        chunks[h, :size, :] = cot[:, h * head_dim : (h + 1) * head_dim]
        rows = [
            log_sums[r, h : h + 1, k * head_dim : (k + 1) * head_dim]
            for r in range(rounds)
            for k in range(size // head_dim)
        ]
        exact = jnp.concatenate(rows, axis=0)
        high = exact.astype(BF16).astype(F32)
        spare = jnp.zeros((chunks.shape[1] - size - 2 * len(rows), head_dim), F32)
        chunks[h, size:, :] = jnp.concatenate([high, exact - high, spare], axis=0).astype(BF16)


def prepare(tokens, gain, cot, log_sums):
    size, width = tokens.shape
    rounds, heads, _ = log_sums.shape
    head_dim = width // heads
    extra = 2 * rounds * size // head_dim
    extra = (extra + 15) // 16 * 16
    return pl.pallas_call(
        prepare_kernel,
        out_shape=[
            jax.ShapeDtypeStruct(tokens.shape, BF16),
            jax.ShapeDtypeStruct((heads, size + extra, head_dim), BF16),
        ],
        compiler_params=pltpu.CompilerParams(vmem_limit_bytes=LARGE_VMEM_BYTES),
        name="prepare",
    )(tokens, gain, cot, log_sums)


def halves_kernel(first, second, upper, lower):
    upper[...] = first[...]
    lower[...] = second[...]


def halves(first, second):
    rows, width = first.shape
    block = (rows // 2, width)
    return pl.pallas_call(
        halves_kernel,
        grid=(1,),
        out_shape=[jax.ShapeDtypeStruct(block, first.dtype)] * 2,
        in_specs=[pl.BlockSpec(block, lambda i: (0, 0)), pl.BlockSpec(block, lambda i: (1, 0))],
        out_specs=[pl.BlockSpec(block, lambda i: (0, 0))] * 2,
        compiler_params=pltpu.CompilerParams(vmem_limit_bytes=SMALL_VMEM_BYTES),
        name="halves",
    )(first, second)


def weight_grad_kernel(per, count, ids, grads, *refs):
    shards = refs[:count]
    outs = refs[count : count + per]
    total = refs[count + per]
    chips, rows, _ = outs[0].shape
    grad_t = jnp.zeros((grads.shape[-1], shards[0].shape[-1]), F32)
    for n, shard in enumerate(shards):
        grad_t = grad_t + dot(grads[ids[SHARDS, n]], shard[...], TN)
    total[...] = grad_t.T
    for m in range(per):
        for k in range(chips):
            chip = lax.rem(ids[SHARDS, 0] + k, chips)
            start = pl.multiple_of((chip * per + ids[LANES, m]) * rows, rows)
            outs[m][k] = total[pl.ds(start, rows), :].astype(BF16)


def weight_grad(per, rows, ids, grads, shards):
    chips, _, both = grads.shape
    smem = pl.BlockSpec(memory_space=pltpu.SMEM)
    vmem = pl.BlockSpec(memory_space=pltpu.VMEM)
    return pl.pallas_call(
        partial(weight_grad_kernel, per, len(shards)),
        out_shape=[jax.ShapeDtypeStruct((chips, rows, both), BF16)] * per,
        in_specs=[smem] + [vmem] * (1 + len(shards)),
        out_specs=[vmem] * per,
        scratch_shapes=[pltpu.VMEM((shards[0].shape[1], both), F32)],
        compiler_params=pltpu.CompilerParams(vmem_limit_bytes=LARGE_VMEM_BYTES),
        name="weight_grad",
    )(ids, grads, *shards)


def home_kernel(grads, w_qk, w_v, tokens, gain, out):
    heads, _, both = grads.shape
    head_dim = both // 2
    total = jnp.zeros(tokens.shape, F32)
    for k in range(heads):
        columns = slice(k * head_dim, (k + 1) * head_dim)
        weights = jnp.concatenate([w_qk[:, columns], w_v[:, columns]], axis=1)
        total = total + dot(grads[k], weights, NT)
    x = tokens[...].astype(F32)
    scale = lax.rsqrt(jnp.mean(x * x, axis=-1, keepdims=True) + EPS)
    scaled = total * gain[...]
    inner = jnp.mean(x * scaled, axis=-1, keepdims=True)
    out[...] = (scale * (scaled - x * (scale * scale * inner))).astype(BF16)


def home(grads, w_qk, w_v, tokens, gain):
    return pl.pallas_call(
        home_kernel,
        out_shape=jax.ShapeDtypeStruct(tokens.shape, BF16),
        compiler_params=pltpu.CompilerParams(vmem_limit_bytes=SMALL_VMEM_BYTES),
        name="home",
    )(grads, w_qk, w_v, tokens, gain)


def rows_kernel(scale_out, ids, qk_own, v_own, own_gain, *refs):
    d_rows = refs[:-3]
    d_wqk, d_wv, d_gain = refs[-3:]
    heads = len(d_rows)
    rows, both = d_rows[0].shape
    head_dim = both // 2
    gains = jnp.zeros((rows, head_dim), F32)
    for k in range(heads):
        source = lax.rem(ids[SHARDS, 0] + heads - k, heads)
        columns = pl.ds(pl.multiple_of(source * head_dim, head_dim), head_dim)
        qk_rows = d_rows[k][:, :head_dim].astype(F32) * scale_out
        v_rows = d_rows[k][:, head_dim:].astype(F32) * scale_out
        d_wqk[:, columns] = qk_rows
        d_wv[:, columns] = v_rows
        gains = gains + qk_rows * qk_own[:, columns].astype(F32)
        gains = gains + v_rows * v_own[:, columns].astype(F32)
    d_gain[...] = jnp.sum(gains.T, axis=0, keepdims=True) / own_gain[...]


def weight_rows(scale_out, ids, d_rows, qk_own, v_own, own_gain):
    rows, width = qk_own.shape
    smem = pl.BlockSpec(memory_space=pltpu.SMEM)
    vmem = pl.BlockSpec(memory_space=pltpu.VMEM)
    return pl.pallas_call(
        partial(rows_kernel, scale_out),
        out_shape=[
            jax.ShapeDtypeStruct((rows, width), F32),
            jax.ShapeDtypeStruct((rows, width), F32),
            jax.ShapeDtypeStruct((1, rows), F32),
        ],
        in_specs=[smem] + [vmem] * (3 + len(d_rows)),
        out_specs=[vmem] * 3,
        compiler_params=pltpu.CompilerParams(vmem_limit_bytes=SMALL_VMEM_BYTES),
        name="weight_rows",
    )(ids, qk_own, v_own, own_gain, *d_rows)


def tables(devices, per, rounds, ring, block_total):
    chips = len(ring)
    place = [ring.index(c) for c in range(chips)]
    steps = [0]
    for s in range(1, chips // 2):
        steps += [-s, s]
    steps.append(chips // 2)
    out = np.zeros((devices, 2, max(chips, per + 3)), np.int32)
    for me in range(devices):
        chip, lane = me // per, me % per
        out[me, SHARDS, :chips] = [ring[(place[chip] + s) % chips] for s in steps]
        out[me, LANES, :per] = [(lane - m) % per for m in range(per)]
        out[me, LANES, per] = lane % rounds
        out[me, LANES, per + 1] = lane // rounds * (block_total * rounds // per)
        out[me, LANES, -1] = me
    return out


def per_device(tokens, norm_gain, w_qk, w_v, cotangent, log_sums, bucket_order, token_position):
    devices = lax.axis_size("tok")
    me = lax.axis_index("tok")
    size, width = tokens.shape
    rounds, heads, _ = log_sums.shape
    head_dim = width // heads
    total = bucket_order.shape[1]
    per = devices // heads
    parts = per // rounds
    chips = heads
    chip, lane = me // per, me % per
    groups = [[c * per + j for c in range(chips)] for j in range(per)]
    ring = list(range(0, chips, 2)) + list(range(chips - 1, 0, -2))

    def hop(x, distance):
        route = [
            (ring[p] * per + j, ring[(p + distance) % chips] * per + j)
            for p in range(chips)
            for j in range(per)
        ]
        return lax.ppermute(x, "tok", route)

    def swap(x, shift):
        route = [
            (c * per + j, c * per + (j + shift) % per) for c in range(chips) for j in range(per)
        ]
        return lax.ppermute(x, "tok", route)

    def send(x, distance):
        route = [
            (c * per + j, (c + distance) % chips * per + j) for c in range(chips) for j in range(per)
        ]
        return lax.ppermute(x, "tok", route)

    def exchange(x):
        return lax.all_to_all(x, "tok", 0, 0, tiled=True, axis_index_groups=groups)

    ids = lax.dynamic_index_in_dim(
        jnp.asarray(tables(devices, per, rounds, ring, total // BLOCK)), me, 0, keepdims=False
    )
    my_order = PITCH * lax.dynamic_index_in_dim(bucket_order, lane % rounds, 0, keepdims=False)
    gain_row = norm_gain[None, :]
    normal, chunks = prepare(tokens, gain_row, cotangent, log_sums)

    shards = [normal]
    ahead = behind = normal
    half = chips // 2
    for s in range(1, half):
        ahead, behind = hop(ahead, 1), hop(behind, -1)
        shards += [ahead, behind]
    upper, lower = halves(ahead, behind)
    shards.append(
        jnp.concatenate([hop(upper, 1), hop(lower, -1)], axis=0)
    )
    cot = exchange(chunks)

    def my_columns(w):
        return lax.dynamic_slice_in_dim(w, chip * head_dim, head_dim, 1)

    my_weights = jnp.concatenate([my_columns(w_qk), my_columns(w_v)], axis=1)

    rows = width // devices
    qk_own, v_own, own_gain = [
        lax.dynamic_slice_in_dim(v, me * rows, rows, 0) for v in (w_qk, w_v, norm_gain)
    ]
    shards[0], ids, my_order, qk_own, v_own, own_gain = lax.optimization_barrier(
        (shards[0], ids, my_order, qk_own, v_own, own_gain)
    )

    def project(some):
        return jnp.stack(
            [jnp.dot(n, my_weights, preferred_element_type=F32).astype(BF16) for n in some]
        )

    early = chips - 3
    qv = [project(shards[:early]), project(shards[early:-1]), project(shards[-1:])]
    qv_all = [qv] + [[swap(x, shift) for x in qv] for shift in range(1, per)]
    cot_all = [cot] + [swap(cot, shift) for shift in range(1, per)]
    sent = attention(per, parts, rounds, ids, my_order, qv_all, cot_all)
    grads = sent[0].astype(F32)
    for shift in range(1, per):
        grads = grads + swap(sent[shift], per - shift).astype(F32)
    grads = grads.astype(BF16)
    inbound = exchange(grads)
    partials = weight_grad(per, rows, ids, grads, shards)
    mine = partials[0].astype(F32)
    for shift in range(1, per):
        mine = mine + swap(partials[shift], per - shift).astype(F32)
    mine = mine.astype(BF16)
    d_rows = [mine[0]] + [send(mine[k], k) for k in range(1, chips)]
    d_tokens = home(inbound, w_qk, w_v, tokens, gain_row)
    *d_rows, d_tokens = lax.optimization_barrier((*d_rows, d_tokens))
    d_wqk, d_wv, d_gain = weight_rows(
        1.0 / math.sqrt(total), ids, d_rows, qk_own, v_own, own_gain[None, :]
    )
    return d_tokens, d_gain.reshape(rows), d_wqk, d_wv


def solution(mesh):
    in_specs = (
        P(("groups", "tok"), None),
        P(),
        P(),
        P(),
        P(("groups", "tok"), None),
        P(None, None, ("groups", "tok")),
        P(None, "groups"),
        P(None, ("groups", "tok")),
    )
    out_specs = (
        P(("groups", "tok"), None),
        P(("groups", "tok")),
        P(("groups", "tok"), None),
        P(("groups", "tok"), None),
    )
    return jax.shard_map(
        per_device, mesh=mesh, in_specs=in_specs, out_specs=out_specs, check_vma=False
    )
```
